512 devices in a mesh: loop: 16 (over x, y_hi, core), out: 32 (over z, y_lo).
Axes of the slice: x: 4, y: 4 (y_hi: 2, y_lo: 2; y = y_hi * 2 + y_lo), z: 16, core: 2. Of those that a mesh axis runs over, the one named last changes fastest.
Arguments:
- activations: bfloat16 [10, 128, 8192], P(None, 'loop'), may hold values from -6 to 6
- out_grads: bfloat16 [10, 128, 28672], P(None, 'loop', 'out'), may hold values from -6 to 6
- token_counts: int32 [10], replicated, may hold values from 1 to 128, 800 in all
- basis_in: bfloat16 [8192, 8192], P('loop', 'out'), may hold values from -0.0625 to 0.0625
- basis_out: bfloat16 [28672, 14336], P('out', 'loop'), may hold values from -0.03125 to 0.03125
- eigenvalues: float32 [14336, 8192], P('loop', 'out'), may hold values from 0.05 to 5
Outputs:
- scaled_queries: bfloat16 [2, 14336, 8192], P(None, 'loop', 'out')
- scores: float32 [2, 8], replicated
The draws below stay inside these ranges and needn't reach their ends.
Inputs may be any that keep to these rules, and one draw needn't show every extreme that they name: `token_counts`: the counts sum to exactly 800, and the largest count is exactly 128.
All inputs are finite; a program needn't handle non-finite values.
Results may differ from the reference program's by a relative error of at most 0.0057.
Values may be sent and summed in bfloat16 or wider, within the bound.
A program may use at most 128 MiB of HBM per device.

```python
import math
import jax
import jax.numpy as jnp
import numpy as np

DIN = 8192
DOUT = 28672
KS = 14336
LMAX = 128
QUERIES = 2
FORGETS = 8
EXAMPLES = 10


def shard_levels(key, dims, pieces, low, high):
    level = 1.0
    for position, parts in pieces:
        draws = jax.random.uniform(jax.random.fold_in(jax.random.fold_in(key, 6), position), (parts,), jnp.float32, low / len(pieces), high / len(pieces))
        level = level * jnp.repeat(jnp.exp(draws), dims[position] // parts).reshape((-1,) + (1,) * (len(dims) - 1 - position))
    return level


def profile(number_of, total, reach, skew):
    weights = [(1 << 20) // math.isqrt(standing ** skew) + 1 for standing in range(2, number_of + 1)]
    surplus, holding = total - reach - (number_of - 1), [1] * (number_of - 1)
    while surplus > 0:
        movable = [i for i in range(number_of - 1) if holding[i] < reach]
        mass, budget = sum([weights[i] for i in movable]), surplus
        for i in movable:
            addition = min(reach - holding[i], max(1, budget * weights[i] // mass), surplus)
            holding[i] = holding[i] + addition
            surplus = surplus - addition
    return np.array([reach] + holding)


def uneven_parts(stream_key, amount, total, bound, skew):
    if amount == 2:
        one = jax.random.randint(stream_key, (), max(1, total - bound), min(bound, total - 1) + 1)
        return jnp.stack([one, total - one])
    sizes = jnp.asarray(profile(amount, total, bound, skew), jnp.int32)
    couples = (amount - 1) // 2
    donor, receiver = sizes[1:1 + 2 * couples:2], sizes[2:2 + 2 * couples:2]
    room = jnp.minimum(donor - 1, bound - receiver)
    passed = jax.random.randint(jax.random.fold_in(stream_key, 1), (couples,), 0, 1 << 20) % (room + 1)
    sizes = sizes.at[1:1 + 2 * couples:2].set(donor - passed).at[2:2 + 2 * couples:2].set(receiver + passed)
    return sizes[jax.random.permutation(jax.random.fold_in(stream_key, 2), amount)]


def gaussian(own_key, extent, width, reach, cuts=(), kind=jnp.bfloat16):
    values = jax.random.normal(own_key, extent, jnp.float32) * width
    if len(cuts) > 0:
        values = shard_levels(own_key, extent, cuts, -0.22, 0.18) * values
    return jnp.clip(values, min=-reach, max=reach).astype(kind)


def setup_inputs(seed: int = 0) -> dict:
    key_of = jax.random.split(jax.random.key(seed), 7)
    return {
        "activations": gaussian(key_of[0], (EXAMPLES, LMAX, DIN), 1.0, 6.0, ((1, 16),)),
        "out_grads": gaussian(key_of[1], (EXAMPLES, LMAX, DOUT), 1.0, 6.0, ((1, 16), (2, 32))),
        "token_counts": uneven_parts(key_of[2], EXAMPLES, EXAMPLES * LMAX * 5 // 8, LMAX, 2).astype(jnp.int32),
        "basis_in": gaussian(key_of[3], (DIN, DIN), DIN ** -0.5, 0.0625, ((0, 16), (1, 32))),
        "basis_out": gaussian(key_of[4], (DOUT, KS), DOUT ** -0.5, 0.03125, ((0, 32), (1, 16))),
        "eigenvalues": jnp.clip(jnp.exp(math.log(5.0) - 4.6051702 * jax.random.uniform(key_of[5], (KS, DIN), jnp.float32) ** shard_levels(key_of[5], (KS, DIN), ((0, 16), (1, 32)), -0.2, 0.2)), 0.05, 5.0),
    }


damping = 0.1


def reference(activations, out_grads, token_counts, basis_in, basis_out, eigenvalues):
    rot_act = jnp.dot(activations.reshape(EXAMPLES * LMAX, DIN), basis_in, preferred_element_type=jnp.float32)
    rot_act = rot_act.astype(jnp.bfloat16).reshape(EXAMPLES, LMAX, DIN)
    rot_grad = jnp.dot(out_grads.reshape(EXAMPLES * LMAX, DOUT), basis_out, preferred_element_type=jnp.float32)
    rot_grad = rot_grad.astype(jnp.bfloat16).reshape(EXAMPLES, LMAX, KS)
    positions = jnp.arange(LMAX, dtype=jnp.int32)
    valid = (positions[None, :] < token_counts[:, None]).astype(jnp.bfloat16)
    masked = rot_act * valid[:, :, None]
    factor = 1.0 / (LMAX ** 0.5)

    def block(index):
        return jnp.dot(rot_grad[index].T, masked[index], preferred_element_type=jnp.float32) * factor

    divisor = eigenvalues + damping
    scaled = jnp.stack([(block(q) / divisor).astype(jnp.bfloat16) for q in range(QUERIES)])
    wide_scaled = scaled.astype(jnp.float32)
    columns = []
    for f in range(FORGETS):
        forget_block = block(QUERIES + f)
        columns.append(jnp.sum(wide_scaled * forget_block[None], axis=(1, 2)))
    scores = jnp.stack(columns, axis=1) / ((KS * DIN) ** 0.5)
    return scaled, scores
```

```python
import functools

import jax
import jax.numpy as jnp
import numpy as np
from jax import lax
from jax.experimental import pallas as pl
from jax.experimental.pallas import tpu as pltpu
from jax.sharding import PartitionSpec as P

DIN = 8192
KS = 14336
QUERIES = 2
VALID = 800
SUBS = 2
damping = 0.1

F32 = jnp.float32
BF16 = jnp.bfloat16
MESH = pl.DeviceIdType.MESH


def remote(src, dst, send, recv, **where):
    return pltpu.make_async_remote_copy(
        src_ref=src, dst_ref=dst, send_sem=send, recv_sem=recv, device_id=where, device_id_type=MESH
    )


def loop(low, high, body):
    lax.fori_loop(low, high, lambda i, c: (body(i), c)[1], 0)


def kernel(
    d,
    counts, slots, act, grads, basis_in, basis_out, eig,
    scaled_out, scores_out,
    g_all, b_out, onehot, part, rs_first, rs_right, rs_left, y_mine, y_other, rot,
    basis_all, act_all, rot_act, masked, queries, eig_v, scaled, acc, sa, sb,
    loc, g_send, g_recv, f_send, f_recv, b_send, b_recv, a_send, a_recv,
    rs_send, rs_recv, y_send, y_recv, ag_send, ag_recv, ra_send, ra_recv,
    sa_send, sa_recv, sb_send, sb_recv,
):
    L, O, X, Z = d["L"], d["O"], d["X"], d["Z"]
    T, E, rows, CT, QR = d["T"], d["E"], d["rows"], d["CT"], d["QR"]
    CH, SC = d["CH"], d["SC"]
    HR = Z // 2
    HL = Z - 1 - HR
    me_l, me_o = lax.axis_index("loop"), lax.axis_index("out")
    core, yh, x = lax.rem(me_l, 2), lax.rem(me_l // 2, 2), me_l // 4
    z, yl = me_o // 2, lax.rem(me_o, 2)
    partner = me_l + 1 - 2 * core
    y_peer = me_o + 1 - 2 * yl

    def rank(dx, dy, dc):
        return (lax.rem(x + dx, X) * 2 + lax.rem(yh + dy, 2)) * 2 + lax.rem(core + dc, 2)

    def to_loop(r):
        return rank(r // 4, lax.rem(r // 2, 2), lax.rem(r, 2))

    def from_loop(r):
        return rank(X - r // 4, 2 - lax.rem(r // 2, 2), 2 - lax.rem(r, 2))

    def ring(k):
        return lax.rem(z + k + 2 * Z, Z)

    def z_peer(k):
        return ring(k) * 2 + yl

    own_g = pltpu.make_async_copy(grads, g_all.at[me_l], loc.at[0])
    own_act = pltpu.make_async_copy(act, act_all.at[core], loc.at[1])
    own_b = pltpu.make_async_copy(basis_out, b_out, loc.at[2])
    own_eig = pltpu.make_async_copy(eig, eig_v, loc.at[3])
    half = basis_all.shape[2]
    own_basis = pltpu.make_async_copy(
        basis_in.at[:, pl.ds(pl.multiple_of(core * half, half), half)], basis_all.at[me_l], loc.at[4]
    )
    for copy in (own_g, own_b, own_act, own_eig, own_basis):
        copy.start()

    barrier = pltpu.get_barrier_semaphore()
    loop(1, L, lambda r: pl.semaphore_signal(
        barrier, inc=1, device_id={"loop": to_loop(r)}, device_id_type=MESH))
    loop(1, O, lambda k: pl.semaphore_signal(
        barrier, inc=1, device_id={"out": lax.rem(me_o + k, O)}, device_id_type=MESH))
    pl.semaphore_wait(barrier, L + O - 2)

    def g_copy(r):
        return remote(grads, g_all.at[me_l], g_send.at[r], g_recv.at[r], loop=to_loop(2 * r))

    def g_forward(r):
        src = from_loop(2 * r)
        return remote(g_all.at[src], g_all.at[src], f_send.at[r], f_recv.at[r], loop=partner)

    def g_landed(r):
        src = from_loop(2 * r)
        return remote(grads, g_all.at[src], g_send.at[r], g_recv.at[r], loop=partner)

    def g_forwarded(r):
        src = from_loop(2 * r)
        src = src + 1 - 2 * lax.rem(src, 2)
        return remote(grads, g_all.at[src], f_send.at[r], f_recv.at[r], loop=partner)

    shards = L // 2
    loop(1, shards, lambda i: g_copy(shards - i).start())
    remote(grads, g_all.at[me_l], f_send.at[0], f_recv.at[0], loop=partner).start()
    act_copy = remote(act, act_all.at[core], a_send, a_recv, loop=partner)
    act_copy.start()

    which, position = slots[0:1, :], slots[1:2, :]
    target = jnp.full(which.shape, -1, jnp.int32)
    starts = []
    first = jnp.int32(0)
    for e in range(E):
        count = counts[e]
        target = jnp.where((which == e) & (position < count), position + first, target)
        starts.append(first)
        first = first + count
    starts.append(first)
    PB = d["PB"]

    def fill(i):
        at = pl.multiple_of(i * PB, PB)
        row = lax.broadcasted_iota(jnp.int32, (PB, which.shape[1]), 0) + at
        onehot[pl.ds(at, PB), :] = jnp.where(row == target, 1.0, 0.0).astype(BF16)

    loop(0, T // PB, fill)
    if Z * CH > CT * T:
        part[CT * T:, :] = jnp.zeros((Z * CH - CT * T, 128), F32)

    def g_step(r):
        g_landed(r).wait_recv()
        g_forward(r).start()

    loop(1, shards, g_step)

    def basis_copy(r):
        there = lax.rem(core + lax.rem(r, 2), 2)
        return remote(
            basis_in.at[:, pl.ds(pl.multiple_of(there * half, half), half)],
            basis_all.at[me_l], b_send.at[r], b_recv.at[r], loop=to_loop(r))

    def basis_landed(r):
        return remote(basis_all.at[me_l], basis_all.at[from_loop(r)], b_send.at[r], b_recv.at[r], loop=partner)

    loop(1, shards, lambda r: g_copy(r).wait_send())
    loop(1, L, lambda i: basis_copy(L - i).start())

    own_g.wait()
    own_b.wait()
    loop(0, shards, lambda r: g_forwarded(r).wait_recv())

    MB = d["MB"]

    def product(i):
        at = pl.multiple_of(i * MB, MB)
        tall = g_all[...].reshape(L * rows, g_all.shape[2])
        valid = jnp.dot(onehot[pl.ds(at, MB), :], tall, preferred_element_type=F32).astype(BF16)
        y = jnp.dot(valid, b_out[...], preferred_element_type=F32)
        for j in range(CT):
            part[pl.ds(pl.multiple_of(at + j * T, 16), MB), :] = y[:, 128 * j:128 * j + 128]

    loop(0, T // MB, product)

    def rows_of(chunk, u):
        return pl.ds(pl.multiple_of(chunk * CH + u * SC, 16), SC)

    def rs_copy(way, s, u, first=False):
        inbox = rs_right if way == 0 else rs_left
        cut = pl.ds(u * SC, SC)
        source = rs_first.at[way, cut] if first else inbox.at[s - 1, cut]
        k = s * SUBS + u
        return remote(source, inbox.at[s, cut], rs_send.at[way, k], rs_recv.at[way, k],
                      out=z_peer(1 if way == 0 else -1))

    def rs_begin(way, u):
        dest = ring(HR) if way == 0 else ring(-HL)
        rs_first[way, pl.ds(u * SC, SC), :] = part[rows_of(dest, u), :]
        rs_copy(way, 0, u, True).start()

    def rs_step(way, s, u):
        inbox = rs_right if way == 0 else rs_left
        cut = pl.ds(u * SC, SC)
        rs_copy(way, s - 1, u, True).wait_recv()
        dest = ring(HR - s) if way == 0 else ring(s - HL)
        inbox[s - 1, cut, :] = inbox[s - 1, cut, :] + part[rows_of(dest, u), :]
        rs_copy(way, s, u).start()

    for u in range(SUBS):
        rs_begin(0, u)
        if HL:
            rs_begin(1, u)

    def rs_both(s):
        for u in range(SUBS):
            rs_step(0, s, u)
            rs_step(1, s, u)

    loop(1, HL, rs_both)
    for s in range(max(HL, 1), HR):
        for u in range(SUBS):
            rs_step(0, s, u)

    def y_copy(u):
        cut = pl.ds(u * SC, SC)
        return remote(y_mine.at[cut], y_other.at[cut], y_send.at[u], y_recv.at[u], out=y_peer)

    def ag_copy(way, s, u):
        chunk = ring(-s) if way == 0 else ring(s)
        place = rot.at[rows_of(chunk, u)]
        k = s * SUBS + u
        return remote(place, place, ag_send.at[way, k], ag_recv.at[way, k],
                      out=z_peer(1 if way == 0 else -1))

    def ag_landed(way, s, u):
        chunk = ring(-1 - s) if way == 0 else ring(1 + s)
        place = rot.at[rows_of(chunk, u)]
        k = s * SUBS + u
        return remote(place, place, ag_send.at[way, k], ag_recv.at[way, k],
                      out=z_peer(1 if way == 0 else -1))

    for u in range(SUBS):
        cut = pl.ds(u * SC, SC)
        total = part[rows_of(z, u), :]
        if HL:
            rs_copy(1, HL - 1, u, True).wait_recv()
            total = total + rs_left[HL - 1, cut, :]
        rs_copy(0, HR - 1, u, True).wait_recv()
        y_mine[cut, :] = total + rs_right[HR - 1, cut, :]
        y_copy(u).start()
    for u in range(SUBS):
        cut = pl.ds(u * SC, SC)
        y_copy(u).wait_recv()
        rot[rows_of(z, u), :] = (y_mine[cut, :] + y_other[cut, :]).astype(BF16)
        ag_copy(0, 0, u).start()
        if HL:
            ag_copy(1, 0, u).start()

    depth = basis_in.shape[0]
    own_basis.wait()
    own_act.wait()
    act_copy.wait_recv()

    def rotate(r, total):
        src = from_loop(r)

        @pl.when(r > 0)
        def _():
            basis_landed(r).wait_recv()

        a = act_all[:, :, pl.ds(pl.multiple_of(src * depth, depth), depth)].reshape(2 * rows, depth)
        return total + jnp.dot(a, basis_all[src], preferred_element_type=F32)

    def ra_copy(r):
        place = rot_act.at[core, pl.ds(pl.multiple_of((me_l // 2) * 2 * rows, 2 * rows), 2 * rows)]
        return remote(place, place, ra_send.at[r], ra_recv.at[r], loop=to_loop(r))

    def ra_landed(r):
        src = from_loop(r)
        place = rot_act.at[lax.rem(src, 2), pl.ds(pl.multiple_of((src // 2) * 2 * rows, 2 * rows), 2 * rows)]
        return remote(place, place, ra_send.at[r], ra_recv.at[r], loop=partner)

    rotated = jnp.zeros((2 * rows, half), F32)
    for s in range(1, max(HR, 5)):
        if s < 5:
            quarter = L // 4
            rotated = lax.fori_loop((s - 1) * quarter, s * quarter, rotate, rotated)
            if s == 4:
                rot_act[core, pl.ds(pl.multiple_of((me_l // 2) * 2 * rows, 2 * rows), 2 * rows), :] = rotated.astype(BF16)
                loop(1, L, lambda i: ra_copy(L - i).start())
        for u in range(SUBS):
            if s < HR:
                ag_landed(0, s - 1, u).wait_recv()
                ag_copy(0, s, u).start()
            if s < HL:
                ag_landed(1, s - 1, u).wait_recv()
                ag_copy(1, s, u).start()

    loop(1, L, lambda r: ra_landed(r).wait_recv())

    def pick(i):
        at = pl.multiple_of(i * MB, MB)
        for c in range(2):
            masked[pl.ds(at, MB), half * c:half * (c + 1)] = jnp.dot(
                onehot[pl.ds(at, MB), :], rot_act[c], preferred_element_type=F32).astype(BF16)

    loop(0, T // MB, pick)
    row = lax.broadcasted_iota(jnp.int32, (QR, 2 * half), 0)
    top = masked[:QR, :]
    for q in range(QUERIES):
        mine = (row >= starts[q]) & (row < starts[q + 1])
        queries[:, 2 * half * q:2 * half * (q + 1)] = jnp.where(mine, top, jnp.zeros_like(top))
    acc[...] = jnp.zeros_like(acc)
    own_eig.wait()
    for u in range(SUBS):
        if HL:
            ag_landed(1, HL - 1, u).wait_recv()
        ag_landed(0, HR - 1, u).wait_recv()

    factor = 1.0 / d["slots"] ** 0.5
    W = 2 * half

    def finish(j):
        grad = rot[pl.ds(pl.multiple_of(j * T, 16), T), :]
        tile = pl.ds(pl.multiple_of(j * 128, 128), 128)
        outer = lax.dot_general(
            grad[:QR], queries[...], (((0,), (0,)), ((), ())), preferred_element_type=F32) * factor
        divisor = eig_v[tile, :] + damping
        parts = []
        for q in range(QUERIES):
            parts.append((outer[:, W * q:W * (q + 1)] / divisor).astype(BF16))
            scaled[q, tile, :] = parts[q]
        wide = lax.dot_general(
            masked[...], jnp.concatenate(parts, axis=0), (((1,), (1,)), ((), ())), preferred_element_type=F32)
        grad = grad.astype(F32)
        for q in range(QUERIES):
            acc[q] = acc[q] + wide[:, 128 * q:128 * (q + 1)] * grad

    loop(0, CT, finish)
    out_copy = pltpu.make_async_copy(scaled, scaled_out, loc.at[5])
    out_copy.start()

    row = lax.broadcasted_iota(jnp.int32, (T, 128), 0)
    F = E - QUERIES
    for f in range(F):
        mine = (row >= starts[QUERIES + f]) & (row < starts[QUERIES + f + 1])
        for q in range(QUERIES):
            sa[me_l, pl.ds(q * F + f, 1), :] = jnp.sum(jnp.where(mine, acc[q], 0.0), axis=0, keepdims=True)

    def sa_copy(r):
        return remote(sa.at[me_l], sa.at[me_l], sa_send.at[r], sa_recv.at[r], loop=to_loop(r))

    def sa_landed(r):
        src = from_loop(r)
        return remote(sa.at[src], sa.at[src], sa_send.at[r], sa_recv.at[r], loop=partner)

    def sb_copy(k):
        return remote(sb.at[me_o], sb.at[me_o], sb_send.at[k], sb_recv.at[k], out=lax.rem(me_o + k, O))

    def sb_landed(k):
        src = lax.rem(me_o + O - k, O)
        return remote(sb.at[src], sb.at[src], sb_send.at[k], sb_recv.at[k], out=y_peer)

    loop(1, L, lambda r: sa_copy(r).start())
    loop(1, L, lambda r: sa_landed(r).wait_recv())
    sb[me_o] = jnp.sum(sa[...], axis=0)
    loop(1, O, lambda k: sb_copy(k).start())
    loop(1, O, lambda k: sb_landed(k).wait_recv())
    score = jnp.sum(jnp.sum(sb[...], axis=0), axis=1, keepdims=True) * (factor / d["cells"] ** 0.5)
    lane = lax.broadcasted_iota(jnp.int32, (F, F), 1)
    sub = lax.broadcasted_iota(jnp.int32, (F, F), 0)
    for q in range(QUERIES):
        own = jnp.where(lane == sub, score[q * F:(q + 1) * F, :], 0.0)
        scores_out[q:q + 1, :] = jnp.sum(own, axis=0, keepdims=True)

    loop(0, shards, lambda r: g_forward(r).wait_send())
    loop(1, L, lambda r: basis_copy(r).wait_send())
    act_copy.wait_send()
    for way, hops in ((0, HR), (1, HL)):
        for s in range(hops):
            for u in range(SUBS):
                rs_copy(way, s, u, True).wait_send()
                ag_copy(way, s, u).wait_send()
    for u in range(SUBS):
        y_copy(u).wait_send()
    loop(1, L, lambda r: ra_copy(r).wait_send())
    loop(1, L, lambda r: sa_copy(r).wait_send())
    loop(1, O, lambda k: sb_copy(k).wait_send())
    out_copy.wait()


def build(mesh, valid, cells):
    L, O = mesh.shape["loop"], mesh.shape["out"]
    Z = O // 2

    def body(activations, out_grads, token_counts, basis_in, basis_out, eigenvalues):
        E, here, din = activations.shape
        feats, cols = basis_out.shape
        depth, wide = basis_in.shape
        rows = E * here
        slots = here * L
        T, CT = valid, cols // 128
        SC = -(-CT * T // (Z * SUBS * 16)) * 16
        CH = SC * SUBS
        HR = Z // 2
        HL = max(Z - 1 - HR, 1)
        half = wide // 2
        d = dict(L=L, O=O, X=L // 4, Z=Z, T=T, E=E, rows=rows, CT=CT, QR=min(QUERIES * slots, T), CH=CH, SC=SC,
                 PB=80 if T % 80 == 0 else 16, MB=400 if T % 400 == 0 else 16, slots=slots, cells=cells)
        index = np.arange(L * rows)
        table = np.zeros((8, L * rows), np.int32)
        table[0] = index % rows // here
        table[1] = index // rows * here + index % here
        dma = pltpu.SemaphoreType.DMA
        F = E - QUERIES
        scratch = [
            pltpu.VMEM((L, rows, feats), BF16),
            pltpu.VMEM((feats, cols), BF16),
            pltpu.VMEM((T, L * rows), BF16),
            pltpu.VMEM((Z * CH, 128), F32),
            pltpu.VMEM((2, CH, 128), F32),
            pltpu.VMEM((HR, CH, 128), F32),
            pltpu.VMEM((HL, CH, 128), F32),
            pltpu.VMEM((CH, 128), F32),
            pltpu.VMEM((CH, 128), F32),
            pltpu.VMEM((Z * CH, 128), BF16),
            pltpu.VMEM((L, depth, half), BF16),
            pltpu.VMEM((2, rows, din), BF16),
            pltpu.VMEM((2, L * rows, half), BF16),
            pltpu.VMEM((T, wide), BF16),
            pltpu.VMEM((d["QR"], QUERIES * wide), BF16),
            pltpu.VMEM((cols, wide), F32),
            pltpu.VMEM((QUERIES, cols, wide), BF16),
            pltpu.VMEM((QUERIES, T, 128), F32),
            pltpu.VMEM((L, QUERIES * F, 128), F32),
            pltpu.VMEM((O, QUERIES * F, 128), F32),
            dma((6,)),
            dma((L // 2,)), dma((L // 2,)), dma((L // 2,)), dma((L // 2,)),
            dma((L,)), dma((L,)), dma, dma,
            dma((2, HR * SUBS)), dma((2, HR * SUBS)), dma((SUBS,)), dma((SUBS,)),
            dma((2, HR * SUBS)), dma((2, HR * SUBS)),
            dma((L,)), dma((L,)), dma((L,)), dma((L,)), dma((O,)), dma((O,)),
        ]
        hbm = pl.BlockSpec(memory_space=pl.ANY)
        vmem = pl.BlockSpec(memory_space=pltpu.VMEM)
        return pl.pallas_call(
            functools.partial(kernel, d),
            out_shape=(
                jax.ShapeDtypeStruct((QUERIES, cols, wide), BF16),
                jax.ShapeDtypeStruct((QUERIES, F), F32),
            ),
            in_specs=[pl.BlockSpec(memory_space=pltpu.SMEM), vmem, hbm, hbm, hbm, hbm, hbm],
            out_specs=(hbm, vmem),
            scratch_shapes=scratch,
            compiler_params=pltpu.CompilerParams(
                collective_id=0, has_side_effects=True, vmem_limit_bytes=56 * 1024 * 1024),
            cost_estimate=pl.CostEstimate(flops=6 * 10**9, bytes_accessed=6 * 10**6, transcendentals=0),
        )(token_counts, jnp.asarray(table), activations.reshape(rows, din), out_grads.reshape(rows, feats),
          basis_in, basis_out, eigenvalues)

    return jax.shard_map(
        body,
        mesh=mesh,
        in_specs=(
            P(None, "loop", None),
            P(None, "loop", "out"),
            P(),
            P("loop", "out"),
            P("out", "loop"),
            P("loop", "out"),
        ),
        out_specs=(P(None, "loop", "out"), P()),
        check_vma=False,
    )


def solution(mesh):
    return build(mesh, VALID, KS * DIN)
```

```python
import functools

import jax
import jax.numpy as jnp
import numpy as np
from jax import lax
from jax.experimental import pallas as pl
from jax.experimental.pallas import tpu as pltpu
from jax.sharding import PartitionSpec as P

DIN = 8192
KS = 14336
QUERIES = 2
VALID = 800
PIECES = 4
damping = 0.1

F32 = jnp.float32
BF16 = jnp.bfloat16
MESH = pl.DeviceIdType.MESH


def remote(src, dst, send, recv, **where):
    return pltpu.make_async_remote_copy(
        src_ref=src, dst_ref=dst, send_sem=send, recv_sem=recv, device_id=where, device_id_type=MESH
    )


def loop(low, high, body):
    lax.fori_loop(low, high, lambda i, c: (body(i), c)[1], 0)


def kernel(
    d,
    counts, slots, act, grads, basis_in, basis_out, eig,
    scaled_out, scores_out,
    g_all, b_out, onehot, part, rs_first, rs_right, rs_left, y_mine, y_other, rot,
    basis_all, act_all, rot_act, masked, queries, eig_v, scaled, acc, sa, sb,
    loc, g_send, g_recv, f_send, f_recv, b_send, b_recv, a_send, a_recv,
    rs_send, rs_recv, y_send, y_recv, ag_send, ag_recv, ra_send, ra_recv,
    sa_send, sa_recv, sb_send, sb_recv,
):
    L, O, X, Z = d["L"], d["O"], d["X"], d["Z"]
    T, E, rows, CT, QR = d["T"], d["E"], d["rows"], d["CT"], d["QR"]
    CH, cuts = d["CH"], d["cuts"]
    F = E - QUERIES
    N = len(cuts)
    HR = Z // 2
    HL = Z - 1 - HR
    me_l, me_o = lax.axis_index("loop"), lax.axis_index("out")
    chip, x = me_l // 2, me_l // 4
    core, yh = me_l - 2 * chip, chip - 2 * x
    z = me_o // 2
    yl = me_o - 2 * z
    partner = me_l + 1 - 2 * core
    y_peer = me_o + 1 - 2 * yl

    def wrap(v, n):
        return jnp.where(v >= n, v - n, v)

    xs = [wrap(x + k, X) for k in range(X)]
    ys = [yh, 1 - yh]
    cs = [core, 1 - core]

    def to_loop(r):
        return (xs[r // 4] * 2 + ys[r // 2 % 2]) * 2 + cs[r % 2]

    def from_loop(r):
        return (xs[-(r // 4) % X] * 2 + ys[r // 2 % 2]) * 2 + cs[r % 2]

    def ring(k):
        v = z + k
        return wrap(jnp.where(v < 0, v + Z, v), Z)

    sides = [ring(1) * 2 + yl, ring(-1) * 2 + yl]
    outs = [wrap(me_o + k, O) for k in range(O)]

    own_g = pltpu.make_async_copy(grads, g_all.at[me_l], loc.at[0])
    own_act = pltpu.make_async_copy(act, act_all.at[core], loc.at[1])
    own_b = pltpu.make_async_copy(basis_out, b_out, loc.at[2])
    own_eig = pltpu.make_async_copy(eig, eig_v, loc.at[3])
    half = basis_all.shape[2]

    def columns(c):
        return pl.ds(pl.multiple_of(c * half, half), half)

    own_basis = pltpu.make_async_copy(basis_in.at[:, columns(core)], basis_all.at[me_l], loc.at[4])

    barrier = pltpu.get_barrier_semaphore()
    for r in range(1, L):
        pl.semaphore_signal(barrier, inc=1, device_id={"loop": to_loop(r)}, device_id_type=MESH)
    for k in range(1, O):
        pl.semaphore_signal(barrier, inc=1, device_id={"out": outs[k]}, device_id_type=MESH)
    for copy in (own_g, own_b, own_act, own_eig, own_basis):
        copy.start()
    pl.semaphore_wait(barrier, L + O - 2)

    shards = L // 2

    def g_copy(r):
        return remote(grads, g_all.at[me_l], g_send, g_recv.at[r], loop=to_loop(2 * r))

    def g_landed(r):
        return remote(grads, g_all.at[from_loop(2 * r)], g_send, g_recv.at[r], loop=partner)

    def g_forward(r):
        src = from_loop(2 * r)
        return remote(g_all.at[src], g_all.at[src], f_send, f_recv, loop=partner)

    for r in range(shards - 1, 0, -1):
        g_copy(r).start()
    remote(grads, g_all.at[me_l], f_send, f_recv, loop=partner).start()
    act_copy = remote(act, act_all.at[core], a_send, a_recv, loop=partner)
    act_copy.start()

    which, position = slots[0:1, :], slots[1:2, :]
    target = jnp.full(which.shape, -1, jnp.int32)
    starts = []
    first = jnp.int32(0)
    for e in range(E):
        count = counts[e]
        target = jnp.where((which == e) & (position < count), position + first, target)
        starts.append(first)
        first = first + count
    starts.append(first)
    PB = d["PB"]

    def fill(i):
        at = pl.multiple_of(i * PB, PB)
        row = lax.broadcasted_iota(jnp.int32, (PB, which.shape[1]), 0) + at
        onehot[pl.ds(at, PB), :] = jnp.where(row == target, 1.0, 0.0).astype(BF16)

    loop(0, T // PB, fill)
    if Z * CH > CT * T:
        part[CT * T:, :] = jnp.zeros((Z * CH - CT * T, 128), F32)

    for r in range(1, shards):
        g_landed(r).wait_recv()
        g_forward(r).start()

    def basis_copy(r):
        return remote(basis_in.at[:, columns(cs[r % 2])], basis_all.at[me_l], b_send, b_recv.at[r], loop=to_loop(r))

    def basis_landed(r):
        src = from_loop(r)
        return remote(basis_all.at[src], basis_all.at[src], b_send, b_recv.at[r], loop=partner)

    def whole(ref, send, recv):
        return remote(ref, ref, send, recv, loop=partner)

    g_sent = whole(g_all.at[pl.ds(0, shards - 1)], g_send, g_recv.at[0])
    forwards = whole(g_all.at[pl.ds(0, shards)], f_send, f_recv)
    if shards > 1:
        g_sent.wait_send()
    for r in range(L - 1, 0, -1):
        basis_copy(r).start()

    own_g.wait()
    own_b.wait()
    forwards.wait_recv()

    MB = d["MB"]

    def product(i):
        at = pl.multiple_of(i * MB, MB)
        tall = g_all[...].reshape(L * rows, g_all.shape[2])
        valid = jnp.dot(onehot[pl.ds(at, MB), :], tall, preferred_element_type=F32).astype(BF16)
        y = jnp.dot(valid, b_out[...], preferred_element_type=F32)
        for j in range(CT):
            part[pl.ds(pl.multiple_of(at + j * T, 16), MB), :] = y[:, 128 * j:128 * j + 128]

    loop(0, T // MB, product)

    inboxes = (rs_right, rs_left)

    def rows_of(chunk, u):
        return pl.ds(pl.multiple_of(chunk * CH + cuts[u][0], 16), cuts[u][1])

    def rs_copy(way, s, u):
        cut = pl.ds(*cuts[u])
        source = rs_first.at[way, cut] if s == 0 else inboxes[way].at[s - 1, cut]
        return remote(source, inboxes[way].at[s, cut], rs_send.at[way], rs_recv.at[way, s * N + u], out=sides[way])

    def rs_step(way, s, u):
        cut = pl.ds(*cuts[u])
        dest = rows_of(ring(HR - s) if way == 0 else ring(s - HL), u)
        if s == 0:
            rs_first[way, cut, :] = part[dest, :]
        else:
            rs_copy(way, s - 1, u).wait_recv()
            inboxes[way][s - 1, cut, :] = inboxes[way][s - 1, cut, :] + part[dest, :]
        rs_copy(way, s, u).start()

    depth = basis_in.shape[0]
    order = [0] + list(range(L - 1, 0, -1))
    rotated = [jnp.zeros((2 * rows, half), F32)]

    def rotate():
        r = order.pop(0)
        if r == 0:
            own_basis.wait()
            own_act.wait()
            act_copy.wait_recv()
        else:
            basis_landed(r).wait_recv()
        src = from_loop(r)
        a = act_all[:, :, pl.ds(pl.multiple_of(src * depth, depth), depth)].reshape(2 * rows, depth)
        rotated[0] = rotated[0] + jnp.dot(a, basis_all[src], preferred_element_type=F32)

    def ra_copy(r):
        place = rot_act.at[core * shards + chip]
        return remote(place, place, ra_send, ra_recv, loop=to_loop(r))

    late = max(HR - -(-L // N), 0)
    for s in range(HR):
        for u in range(N):
            rs_step(0, s, u)
            if s < HL:
                rs_step(1, s, u)
            if s >= late and order:
                rotate()
    while order:
        rotate()
    rot_act[core * shards + chip] = rotated[0].astype(BF16)
    for r in range(L - 1, 0, -1):
        ra_copy(r).start()
    rotations = whole(rot_act.at[pl.ds(0, L - 1)], ra_send, ra_recv)

    def y_copy(u):
        cut = pl.ds(*cuts[u])
        return remote(y_mine.at[cut], y_other.at[cut], y_send.at[u], y_recv.at[u], out=y_peer)

    def ag_copy(way, s, u):
        place = rot.at[rows_of(ring(-s) if way == 0 else ring(s), u)]
        return remote(place, place, ag_send.at[way], ag_recv.at[way, s * N + u], out=sides[way])

    def ag_landed(way, s, u):
        place = rot.at[rows_of(ring(-1 - s) if way == 0 else ring(1 + s), u)]
        return remote(place, place, ag_send.at[way], ag_recv.at[way, s * N + u], out=sides[way])

    for u in range(N):
        cut = pl.ds(*cuts[u])
        total = part[rows_of(z, u), :]
        if HL:
            rs_copy(1, HL - 1, u).wait_recv()
            total = total + rs_left[HL - 1, cut, :]
        rs_copy(0, HR - 1, u).wait_recv()
        y_mine[cut, :] = total + rs_right[HR - 1, cut, :]
        y_copy(u).start()
    for u in range(N):
        cut = pl.ds(*cuts[u])
        y_copy(u).wait_recv()
        rot[rows_of(z, u), :] = (y_mine[cut, :] + y_other[cut, :]).astype(BF16)
        ag_copy(0, 0, u).start()
        if HL:
            ag_copy(1, 0, u).start()

    def gather_valid():
        rotations.wait_recv()

        def pick(i):
            at = pl.multiple_of(i * MB, MB)
            for c in range(2):
                panels = rot_act[shards * c:shards * (c + 1)].reshape(L * rows, half)
                masked[pl.ds(at, MB), half * c:half * (c + 1)] = jnp.dot(
                    onehot[pl.ds(at, MB), :], panels, preferred_element_type=F32).astype(BF16)

        loop(0, T // MB, pick)
        row = lax.broadcasted_iota(jnp.int32, (QR, 2 * half), 0)
        top = masked[:QR, :]
        for q in range(QUERIES):
            own = (row >= starts[q]) & (row < starts[q + 1])
            queries[:, 2 * half * q:2 * half * (q + 1)] = jnp.where(own, top, jnp.zeros_like(top))
        acc[...] = jnp.zeros_like(acc)
        own_eig.wait()

    factor = 1.0 / d["slots"] ** 0.5
    W = 2 * half

    def finish(j):
        grad = rot[pl.ds(pl.multiple_of(j * T, 16), T), :]
        tile = pl.ds(pl.multiple_of(j * 128, 128), 128)
        outer = lax.dot_general(
            grad[:QR], queries[...], (((0,), (0,)), ((), ())), preferred_element_type=F32) * factor
        divisor = eig_v[tile, :] + damping
        parts = []
        for q in range(QUERIES):
            parts.append((outer[:, W * q:W * (q + 1)] / divisor).astype(BF16))
            scaled[q, tile, :] = parts[q]
        wide = lax.dot_general(
            masked[...], jnp.concatenate(parts, axis=0), (((1,), (1,)), ((), ())), preferred_element_type=F32)
        grad = grad.astype(F32)
        for q in range(QUERIES):
            acc[q] = acc[q] + wide[:, 128 * q:128 * (q + 1)] * grad

    first_hop = min(3, HR)

    def complete(j):
        low, high = (j * T) // CH, (j * T + T - 1) // CH
        last = jnp.int32(first_hop)
        for k in range((T - 2) // CH + 2):
            chunk = jnp.minimum(low + k, high)
            ahead = chunk - z
            ahead = jnp.where(ahead < 0, ahead + Z, ahead)
            last = jnp.maximum(last, jnp.where(ahead <= HL, ahead, Z - ahead))
        return last

    for s in range(1, HR + 1):
        for u in range(N):
            ag_landed(0, s - 1, u).wait_recv()
            if s < HR:
                ag_copy(0, s, u).start()
            if s <= HL:
                ag_landed(1, s - 1, u).wait_recv()
                if s < HL:
                    ag_copy(1, s, u).start()
        if s == min(2, HR):
            gather_valid()
        if s >= first_hop:

            def ready(j):
                @pl.when(complete(j) == s)
                def _():
                    finish(j)

            loop(0, CT, ready)

    out_copy = pltpu.make_async_copy(scaled, scaled_out, loc.at[5])
    out_copy.start()

    row = lax.broadcasted_iota(jnp.int32, (T, 128), 0)
    lane = lax.broadcasted_iota(jnp.int32, (1, 128), 1)
    mine = [jnp.zeros((1, 128), F32) for q in range(QUERIES)]
    for f in range(F):
        own = (row >= starts[QUERIES + f]) & (row < starts[QUERIES + f + 1])
        for q in range(QUERIES):
            value = jnp.sum(jnp.sum(jnp.where(own, acc[q], 0.0), axis=0, keepdims=True), axis=1, keepdims=True)
            mine[q] = jnp.where(lane == f, value, mine[q])
    for q in range(QUERIES):
        sa[me_l, q:q + 1, :] = mine[q]

    for r in range(L - 1, 0, -1):
        remote(sa.at[me_l], sa.at[me_l], sa_send, sa_recv, loop=to_loop(r)).start()

    forwards.wait_send()
    whole(basis_all.at[pl.ds(0, L - 1)], b_send, b_recv.at[0]).wait_send()
    act_copy.wait_send()
    for way, hops in ((0, HR), (1, HL)):
        if hops:
            whole(inboxes[way].at[pl.ds(0, hops)], rs_send.at[way], rs_recv.at[way, 0]).wait_send()
            whole(rot.at[pl.ds(0, hops * CH)], ag_send.at[way], ag_recv.at[way, 0]).wait_send()
    for u in range(N):
        y_copy(u).wait_send()
    rotations.wait_send()

    sa_all = whole(sa.at[pl.ds(0, L - 1)], sa_send, sa_recv)
    sa_all.wait_recv()
    sb[me_o] = jnp.sum(sa[...], axis=0)
    for k in range(1, O):
        remote(sb.at[me_o], sb.at[me_o], sb_send, sb_recv, out=outs[k]).start()
    sa_all.wait_send()
    out_copy.wait()
    sb_all = whole(sb.at[pl.ds(0, O - 1)], sb_send, sb_recv)
    sb_all.wait_recv()
    total = jnp.sum(sb[...], axis=0) * (factor / d["cells"] ** 0.5)
    scores_out[...] = total[:, :F]
    sb_all.wait_send()


def build(mesh, valid, cells):
    L, O = mesh.shape["loop"], mesh.shape["out"]
    Z = O // 2

    def body(activations, out_grads, token_counts, basis_in, basis_out, eigenvalues):
        E, here, din = activations.shape
        feats, cols = basis_out.shape
        depth, wide = basis_in.shape
        rows = E * here
        slots = here * L
        T, CT = valid, cols // 128
        groups = -(-CT * T // (Z * 16))
        CH = groups * 16
        edges = [groups * u // PIECES * 16 for u in range(PIECES + 1)]
        cuts = [(a, b - a) for a, b in zip(edges, edges[1:]) if b > a]
        N = len(cuts)
        HR = Z // 2
        HL = max(Z - 1 - HR, 1)
        half = wide // 2
        d = dict(L=L, O=O, X=L // 4, Z=Z, T=T, E=E, rows=rows, CT=CT, QR=min(QUERIES * slots, T), CH=CH, cuts=cuts,
                 PB=80 if T % 80 == 0 else 16, MB=400 if T % 400 == 0 else 16, slots=slots, cells=cells)
        index = np.arange(L * rows)
        table = np.zeros((8, L * rows), np.int32)
        table[0] = index % rows // here
        table[1] = index // rows * here + index % here
        dma = pltpu.SemaphoreType.DMA
        F = E - QUERIES
        scratch = [
            pltpu.VMEM((L, rows, feats), BF16),
            pltpu.VMEM((feats, cols), BF16),
            pltpu.VMEM((T, L * rows), BF16),
            pltpu.VMEM((Z * CH, 128), F32),
            pltpu.VMEM((2, CH, 128), F32),
            pltpu.VMEM((HR, CH, 128), F32),
            pltpu.VMEM((HL, CH, 128), F32),
            pltpu.VMEM((CH, 128), F32),
            pltpu.VMEM((CH, 128), F32),
            pltpu.VMEM((Z * CH, 128), BF16),
            pltpu.VMEM((L, depth, half), BF16),
            pltpu.VMEM((2, rows, din), BF16),
            pltpu.VMEM((L, 2 * rows, half), BF16),
            pltpu.VMEM((T, wide), BF16),
            pltpu.VMEM((d["QR"], QUERIES * wide), BF16),
            pltpu.VMEM((cols, wide), F32),
            pltpu.VMEM((QUERIES, cols, wide), BF16),
            pltpu.VMEM((QUERIES, T, 128), F32),
            pltpu.VMEM((L, QUERIES, 128), F32),
            pltpu.VMEM((O, QUERIES, 128), F32),
            dma((6,)),
            dma, dma((L // 2,)), dma, dma,
            dma, dma((L,)), dma, dma,
            dma((2,)), dma((2, HR * N)), dma((N,)), dma((N,)),
            dma((2,)), dma((2, HR * N)),
            dma, dma, dma, dma, dma, dma,
        ]
        hbm = pl.BlockSpec(memory_space=pl.ANY)
        vmem = pl.BlockSpec(memory_space=pltpu.VMEM)
        return pl.pallas_call(
            functools.partial(kernel, d),
            out_shape=(
                jax.ShapeDtypeStruct((QUERIES, cols, wide), BF16),
                jax.ShapeDtypeStruct((QUERIES, F), F32),
            ),
            in_specs=[pl.BlockSpec(memory_space=pltpu.SMEM), vmem, hbm, hbm, hbm, hbm, hbm],
            out_specs=(hbm, vmem),
            scratch_shapes=scratch,
            compiler_params=pltpu.CompilerParams(
                collective_id=0, has_side_effects=True, vmem_limit_bytes=56 * 1024 * 1024),
            cost_estimate=pl.CostEstimate(flops=6 * 10**9, bytes_accessed=6 * 10**6, transcendentals=0),
        )(token_counts, jnp.asarray(table), activations.reshape(rows, din), out_grads.reshape(rows, feats),
          basis_in, basis_out, eigenvalues)

    return jax.shard_map(
        body,
        mesh=mesh,
        in_specs=(
            P(None, "loop", None),
            P(None, "loop", "out"),
            P(),
            P("loop", "out"),
            P("out", "loop"),
            P("loop", "out"),
        ),
        out_specs=(P(None, "loop", "out"), P()),
        check_vma=False,
    )


def solution(mesh):
    return build(mesh, VALID, KS * DIN)
```

```python
import functools

import jax
import jax.numpy as jnp
import numpy as np
from jax import lax
from jax.experimental import pallas as pl
from jax.experimental.pallas import tpu as pltpu
from jax.sharding import PartitionSpec as P

DIN = 8192
KS = 14336
QUERIES = 2
VALID = 800
PIECES = 4
damping = 0.1

F32 = jnp.float32
BF16 = jnp.bfloat16
MESH = pl.DeviceIdType.MESH


def remote(src, dst, send, recv, **where):
    return pltpu.make_async_remote_copy(
        src_ref=src, dst_ref=dst, send_sem=send, recv_sem=recv, device_id=where, device_id_type=MESH
    )


def loop(low, high, body):
    lax.fori_loop(low, high, lambda i, c: (body(i), c)[1], 0)


def kernel(
    d,
    counts, slots, act, grads, basis_in, basis_out, eig,
    scaled_out, scores_out,
    g_all, b_out, onehot, valid, part, rs_first, rs_right, rs_left, y_mine, y_other, rot,
    basis_all, act_all, rot_act, masked, queries, eig_v, acc, sa, sb,
    loc, g_send, g_recv, f_send, f_recv, b_send, b_recv, a_send, a_recv,
    rs_send, rs_recv, y_send, y_recv, ag_send, ag_recv, ra_send, ra_recv,
    sa_send, sa_recv, sb_send, sb_recv,
):
    L, O, X, Z = d["L"], d["O"], d["X"], d["Z"]
    T, E, rows, CT, QR = d["T"], d["E"], d["rows"], d["CT"], d["QR"]
    CH, cuts = d["CH"], d["cuts"]
    F = E - QUERIES
    N = len(cuts)
    HR = Z // 2
    HL = Z - 1 - HR
    me_l, me_o = lax.axis_index("loop"), lax.axis_index("out")
    chip, x = me_l // 2, me_l // 4
    core, yh = me_l - 2 * chip, chip - 2 * x
    z = me_o // 2
    yl = me_o - 2 * z
    partner = me_l + 1 - 2 * core
    y_peer = me_o + 1 - 2 * yl

    def wrap(v, n):
        return jnp.where(v >= n, v - n, v)

    xs = [wrap(x + k, X) for k in range(X)]
    ys = [yh, 1 - yh]
    cs = [core, 1 - core]

    def to_loop(r):
        return (xs[r // 4] * 2 + ys[r // 2 % 2]) * 2 + cs[r % 2]

    def from_loop(r):
        return (xs[-(r // 4) % X] * 2 + ys[r // 2 % 2]) * 2 + cs[r % 2]

    def ring(k):
        v = z + k
        return wrap(jnp.where(v < 0, v + Z, v), Z)

    sides = [ring(1) * 2 + yl, ring(-1) * 2 + yl]
    outs = [wrap(me_o + k, O) for k in range(O)]

    own_g = pltpu.make_async_copy(grads, g_all.at[me_l], loc.at[0])
    own_act = pltpu.make_async_copy(act, act_all.at[core], loc.at[1])
    own_b = pltpu.make_async_copy(basis_out, b_out, loc.at[2])
    own_eig = pltpu.make_async_copy(eig, eig_v, loc.at[3])
    half = basis_all.shape[2]

    def columns(c):
        return pl.ds(pl.multiple_of(c * half, half), half)

    own_basis = pltpu.make_async_copy(basis_in.at[:, columns(core)], basis_all.at[me_l], loc.at[4])

    barrier = pltpu.get_barrier_semaphore()
    for r in range(1, L):
        pl.semaphore_signal(barrier, inc=1, device_id={"loop": to_loop(r)}, device_id_type=MESH)
    near = sides + [y_peer]
    for peer in near:
        pl.semaphore_signal(barrier, inc=1, device_id={"out": peer}, device_id_type=MESH)
    for copy in (own_g, own_b, own_act, own_eig, own_basis):
        copy.start()
    pl.semaphore_wait(barrier, L - 1 + len(near))

    shards = L // 2

    low = rows // 32 * 16
    splits = [(0, low), (low, rows - low)] if low else [(0, rows)]
    G = len(splits)

    def g_copy(r, p):
        cut = pl.ds(*splits[p])
        return remote(grads.at[cut], g_all.at[me_l, cut], g_send, g_recv.at[r, p], loop=to_loop(2 * r))

    def g_landed(r, p):
        here = g_all.at[from_loop(2 * r), pl.ds(*splits[p])]
        return remote(here, here, g_send, g_recv.at[r, p], loop=partner)

    def g_forward(r, p):
        here = g_all.at[from_loop(2 * r), pl.ds(*splits[p])]
        return remote(here, here, f_send, f_recv, loop=partner)

    for p in range(G):
        for r in range(shards - 1, 0, -1):
            g_copy(r, p).start()
    remote(grads, g_all.at[me_l], f_send, f_recv, loop=partner).start()

    which, position = slots[0:1, :], slots[1:2, :]
    target = jnp.full(which.shape, -1, jnp.int32)
    starts = []
    first = jnp.int32(0)
    for e in range(E):
        count = counts[e]
        target = jnp.where((which == e) & (position < count), position + first, target)
        starts.append(first)
        first = first + count
    starts.append(first)
    PB = d["PB"]

    def fill(i):
        at = pl.multiple_of(i * PB, PB)
        row = lax.broadcasted_iota(jnp.int32, (PB, which.shape[1]), 0) + at
        onehot[pl.ds(at, PB), :] = jnp.where(row == target, 1.0, 0.0).astype(BF16)

    loop(0, T // PB, fill)
    if Z * CH > CT * T:
        part[CT * T:, :] = jnp.zeros((Z * CH - CT * T, 128), F32)

    for p in range(G):
        for r in range(shards - 1, 0, -1):
            g_landed(r, p).wait_recv()
            g_forward(r, p).start()

    def basis_copy(r):
        return remote(basis_in.at[:, columns(cs[r % 2])], basis_all.at[me_l], b_send, b_recv.at[r], loop=to_loop(r))

    def basis_landed(r):
        src = from_loop(r)
        return remote(basis_all.at[src], basis_all.at[src], b_send, b_recv.at[r], loop=partner)

    def whole(ref, send, recv):
        return remote(ref, ref, send, recv, loop=partner)

    g_sent = whole(g_all.at[pl.ds(0, shards - 1)], g_send, g_recv.at[0, 0])
    forwards = whole(g_all.at[pl.ds(0, shards)], f_send, f_recv)
    act_copy = remote(act, act_all.at[core], a_send, a_recv, loop=partner)
    act_copy.start()
    if shards > 1:
        g_sent.wait_send()
    for r in range(L - 1, 0, -1):
        basis_copy(r).start()
    own_g.wait()
    forwards.wait_recv()

    MB = d["MB"]

    def compact(i):
        cut = pl.ds(pl.multiple_of(i * MB, MB), MB)
        tall = g_all[...].reshape(L * rows, g_all.shape[2])
        valid[cut, :] = jnp.dot(onehot[cut, :], tall, preferred_element_type=F32).astype(BF16)

    loop(0, T // MB, compact)
    own_b.wait()

    def product(j):
        tile = pl.ds(pl.multiple_of(j * 128, 128), 128)

        def block(i):
            at = pl.multiple_of(i * MB, MB)
            part[pl.ds(pl.multiple_of(j * T + at, 16), MB), :] = jnp.dot(
                valid[pl.ds(at, MB), :], b_out[:, tile], preferred_element_type=F32)

        loop(0, T // MB, block)

    def each_chunk(j, begin, step_of, merge):
        low, high = (j * T) // CH, (j * T + T - 1) // CH
        value = jnp.int32(begin)
        for k in range((T - 2) // CH + 2):
            ahead = jnp.minimum(low + k, high) - z
            value = merge(value, step_of(jnp.where(ahead < 0, ahead + Z, ahead)))
        return value

    def wanted(ahead):
        return jnp.where(ahead == 0, HR, jnp.where(ahead <= HR, HR - ahead, ahead - HR - 1))

    def products(s):
        def when_due(j):
            @pl.when(each_chunk(j, HR, wanted, jnp.minimum) == s)
            def _():
                product(j)

        loop(0, CT, when_due)

    inboxes = (rs_right, rs_left)

    def rows_of(chunk, u):
        return pl.ds(pl.multiple_of(chunk * CH + cuts[u][0], 16), cuts[u][1])

    def rs_copy(way, s, u):
        cut = pl.ds(*cuts[u])
        source = rs_first.at[way, cut] if s == 0 else inboxes[way].at[s - 1, cut]
        return remote(source, inboxes[way].at[s, cut], rs_send.at[way], rs_recv.at[way, s * N + u], out=sides[way])

    def rs_step(way, s, u):
        cut = pl.ds(*cuts[u])
        dest = rows_of(ring(HR - s) if way == 0 else ring(s - HL), u)
        if s == 0:
            rs_first[way, cut, :] = part[dest, :]
        else:
            rs_copy(way, s - 1, u).wait_recv()
            inboxes[way][s - 1, cut, :] = inboxes[way][s - 1, cut, :] + part[dest, :]
        rs_copy(way, s, u).start()

    depth = basis_in.shape[0]
    order = [0] + list(range(L - 1, 0, -1))
    rotated = [jnp.zeros((2 * rows, half), F32)]

    def rotate():
        r = order.pop(0)
        if r == 0:
            own_basis.wait()
            own_act.wait()
            act_copy.wait_recv()
        else:
            basis_landed(r).wait_recv()
        src = from_loop(r)
        a = act_all[:, :, pl.ds(pl.multiple_of(src * depth, depth), depth)].reshape(2 * rows, depth)
        rotated[0] = rotated[0] + jnp.dot(a, basis_all[src], preferred_element_type=F32)

    def ra_copy(r):
        place = rot_act.at[chip, :, columns(core)]
        return remote(place, place, ra_send, ra_recv, loop=to_loop(r))

    products(0)
    late = max(HR - -(-L // (2 * N)), 0)
    for s in range(HR):
        for u in range(N):
            rs_step(0, s, u)
            if s < HL:
                rs_step(1, s, u)
            for _ in range(2):
                if s >= late and order:
                    rotate()
        products(s + 1)
    while order:
        rotate()
    rot_act[chip, :, columns(core)] = rotated[0].astype(BF16)
    for r in range(L - 1, 0, -1):
        ra_copy(r).start()
    rotations = whole(act_all.at[:, :, pl.ds(0, (L - 1) * half)], ra_send, ra_recv)

    def y_copy(u):
        cut = pl.ds(*cuts[u])
        return remote(y_mine.at[cut], y_other.at[cut], y_send.at[u], y_recv.at[u], out=y_peer)

    def ag_copy(way, s, u):
        place = rot.at[rows_of(ring(-s) if way == 0 else ring(s), u)]
        return remote(place, place, ag_send.at[way], ag_recv.at[way, s * N + u], out=sides[way])

    def ag_landed(way, s, u):
        place = rot.at[rows_of(ring(-1 - s) if way == 0 else ring(1 + s), u)]
        return remote(place, place, ag_send.at[way], ag_recv.at[way, s * N + u], out=sides[way])

    for u in range(N):
        cut = pl.ds(*cuts[u])
        total = part[rows_of(z, u), :]
        if HL:
            rs_copy(1, HL - 1, u).wait_recv()
            total = total + rs_left[HL - 1, cut, :]
        rs_copy(0, HR - 1, u).wait_recv()
        y_mine[cut, :] = total + rs_right[HR - 1, cut, :]
        y_copy(u).start()
    for u in range(N):
        cut = pl.ds(*cuts[u])
        y_copy(u).wait_recv()
        rot[rows_of(z, u), :] = (y_mine[cut, :] + y_other[cut, :]).astype(BF16)
        ag_copy(0, 0, u).start()
        if HL:
            ag_copy(1, 0, u).start()

    def gather_valid():
        rotations.wait_recv()

        def pick(i):
            cut = pl.ds(pl.multiple_of(i * MB, MB), MB)
            panels = rot_act[...].reshape(L * rows, 2 * half)
            masked[cut, :] = jnp.dot(onehot[cut, :], panels, preferred_element_type=F32).astype(BF16)

        loop(0, T // MB, pick)
        row = lax.broadcasted_iota(jnp.int32, (QR, 2 * half), 0)
        top = masked[:QR, :]
        for q in range(QUERIES):
            own = (row >= starts[q]) & (row < starts[q + 1])
            queries[:, 2 * half * q:2 * half * (q + 1)] = jnp.where(own, top, jnp.zeros_like(top))
        acc[...] = jnp.zeros_like(acc)
        own_eig.wait()

    factor = 1.0 / d["slots"] ** 0.5
    W = 2 * half

    def finish(j):
        grad = rot[pl.ds(pl.multiple_of(j * T, 16), T), :]
        tile = pl.ds(pl.multiple_of(j * 128, 128), 128)
        outer = lax.dot_general(
            grad[:QR], queries[...], (((0,), (0,)), ((), ())), preferred_element_type=F32) * factor
        divisor = eig_v[tile, :] + damping
        parts = []
        for q in range(QUERIES):
            parts.append((outer[:, W * q:W * (q + 1)] / divisor).astype(BF16))
            scaled_out[q, tile, :] = parts[q]
        wide = lax.dot_general(
            masked[...], jnp.concatenate(parts, axis=0), (((1,), (1,)), ((), ())), preferred_element_type=F32)
        grad = grad.astype(F32)
        for q in range(QUERIES):
            acc[q] = acc[q] + wide[:, 128 * q:128 * (q + 1)] * grad

    first_hop = min(4, HR)

    def arrival(ahead):
        return jnp.where(ahead <= HL, ahead, Z - ahead)

    for s in range(1, HR + 1):
        for u in range(N):
            ag_landed(0, s - 1, u).wait_recv()
            if s < HR:
                ag_copy(0, s, u).start()
            if s <= HL:
                ag_landed(1, s - 1, u).wait_recv()
                if s < HL:
                    ag_copy(1, s, u).start()
        if s == min(3, HR):
            gather_valid()
        if s >= first_hop:

            def ready(j):
                @pl.when(each_chunk(j, first_hop, arrival, jnp.maximum) == s)
                def _():
                    finish(j)

            loop(0, CT, ready)

    row = lax.broadcasted_iota(jnp.int32, (T, 128), 0)
    lane = lax.broadcasted_iota(jnp.int32, (1, 128), 1)
    mine = [jnp.zeros((1, 128), F32) for q in range(QUERIES)]
    for f in range(F):
        own = (row >= starts[QUERIES + f]) & (row < starts[QUERIES + f + 1])
        for q in range(QUERIES):
            value = jnp.sum(jnp.sum(jnp.where(own, acc[q], 0.0), axis=0, keepdims=True), axis=1, keepdims=True)
            mine[q] = jnp.where(lane == f, value, mine[q])
    for q in range(QUERIES):
        sa[me_l, q:q + 1, :] = mine[q]

    for r in range(L - 1, 0, -1):
        remote(sa.at[me_l], sa.at[me_l], sa_send, sa_recv, loop=to_loop(r)).start()

    forwards.wait_send()
    whole(basis_all.at[pl.ds(0, L - 1)], b_send, b_recv.at[0]).wait_send()
    act_copy.wait_send()
    for way, hops in ((0, HR), (1, HL)):
        if hops:
            whole(inboxes[way].at[pl.ds(0, hops)], rs_send.at[way], rs_recv.at[way, 0]).wait_send()
            whole(rot.at[pl.ds(0, hops * CH)], ag_send.at[way], ag_recv.at[way, 0]).wait_send()
    for u in range(N):
        y_copy(u).wait_send()
    rotations.wait_send()

    sa_all = whole(sa.at[pl.ds(0, L - 1)], sa_send, sa_recv)
    sa_all.wait_recv()
    sb[me_o] = jnp.sum(sa[...], axis=0)
    for k in range(1, O):
        remote(sb.at[me_o], sb.at[me_o], sb_send, sb_recv, out=outs[k]).start()
    sa_all.wait_send()
    sb_all = whole(sb.at[pl.ds(0, O - 1)], sb_send, sb_recv)
    sb_all.wait_recv()
    total = jnp.sum(sb[...], axis=0) * (factor / d["cells"] ** 0.5)
    scores_out[...] = total[:, :F]
    sb_all.wait_send()


def build(mesh, valid, cells):
    L, O = mesh.shape["loop"], mesh.shape["out"]
    Z = O // 2

    def body(activations, out_grads, token_counts, basis_in, basis_out, eigenvalues):
        E, here, din = activations.shape
        feats, cols = basis_out.shape
        depth, wide = basis_in.shape
        rows = E * here
        slots = here * L
        T, CT = valid, cols // 128
        groups = -(-CT * T // (Z * 16))
        CH = groups * 16
        edges = [groups * u // PIECES * 16 for u in range(PIECES + 1)]
        cuts = [(a, b - a) for a, b in zip(edges, edges[1:]) if b > a]
        N = len(cuts)
        HR = Z // 2
        HL = max(Z - 1 - HR, 1)
        half = wide // 2
        d = dict(L=L, O=O, X=L // 4, Z=Z, T=T, E=E, rows=rows, CT=CT, QR=min(QUERIES * slots, T), CH=CH, cuts=cuts,
                 PB=80 if T % 80 == 0 else 16, MB=400 if T % 400 == 0 else 16, slots=slots, cells=cells)
        index = np.arange(L * rows)
        table = np.zeros((8, L * rows), np.int32)
        table[0] = index % rows // here
        table[1] = index // rows * here + index % here
        dma = pltpu.SemaphoreType.DMA
        F = E - QUERIES
        scratch = [
            pltpu.VMEM((L, rows, feats), BF16),
            pltpu.VMEM((feats, cols), BF16),
            pltpu.VMEM((T, L * rows), BF16),
            pltpu.VMEM((T, feats), BF16),
            pltpu.VMEM((Z * CH, 128), F32),
            pltpu.VMEM((2, CH, 128), F32),
            pltpu.VMEM((HR, CH, 128), F32),
            pltpu.VMEM((HL, CH, 128), F32),
            pltpu.VMEM((CH, 128), F32),
            pltpu.VMEM((CH, 128), F32),
            pltpu.VMEM((Z * CH, 128), BF16),
            pltpu.VMEM((L, depth, half), BF16),
            pltpu.VMEM((2, rows, din), BF16),
            pltpu.VMEM((L // 2, 2 * rows, wide), BF16),
            pltpu.VMEM((T, wide), BF16),
            pltpu.VMEM((d["QR"], QUERIES * wide), BF16),
            pltpu.VMEM((cols, wide), F32),
            pltpu.VMEM((QUERIES, T, 128), F32),
            pltpu.VMEM((L, QUERIES, 128), F32),
            pltpu.VMEM((O, QUERIES, 128), F32),
            dma((5,)),
            dma, dma((L // 2, 2)), dma, dma,
            dma, dma((L,)), dma, dma,
            dma((2,)), dma((2, HR * N)), dma((N,)), dma((N,)),
            dma((2,)), dma((2, HR * N)),
            dma, dma, dma, dma, dma, dma,
        ]
        hbm = pl.BlockSpec(memory_space=pl.ANY)
        vmem = pl.BlockSpec(memory_space=pltpu.VMEM)
        return pl.pallas_call(
            functools.partial(kernel, d),
            out_shape=(
                pltpu.VMEM((QUERIES, cols, wide), BF16),
                pltpu.VMEM((QUERIES, F), F32),
            ),
            in_specs=[pl.BlockSpec(memory_space=pltpu.SMEM), vmem, hbm, hbm, hbm, hbm, hbm],
            out_specs=(vmem, vmem),
            scratch_shapes=scratch,
            compiler_params=pltpu.CompilerParams(
                collective_id=0, has_side_effects=True, vmem_limit_bytes=56 * 1024 * 1024),
            cost_estimate=pl.CostEstimate(flops=6 * 10**9, bytes_accessed=6 * 10**6, transcendentals=0),
        )(token_counts, jnp.asarray(table), activations.reshape(rows, din), out_grads.reshape(rows, feats),
          basis_in, basis_out, eigenvalues)

    return jax.shard_map(
        body,
        mesh=mesh,
        in_specs=(
            P(None, "loop", None),
            P(None, "loop", "out"),
            P(),
            P("loop", "out"),
            P("out", "loop"),
            P("loop", "out"),
        ),
        out_specs=(P(None, "loop", "out"), P()),
        check_vma=False,
    )


def solution(mesh):
    return build(mesh, VALID, KS * DIN)
```

```python
import functools

import jax
import jax.numpy as jnp
import numpy as np
from jax import lax
from jax.experimental import pallas as pl
from jax.experimental.pallas import tpu as pltpu
from jax.sharding import PartitionSpec as P

DIN = 8192
KS = 14336
QUERIES = 2
VALID = 800
PIECES = 4
damping = 0.1

F32 = jnp.float32
BF16 = jnp.bfloat16
MESH = pl.DeviceIdType.MESH


def remote(src, dst, send, recv, **where):
    return pltpu.make_async_remote_copy(
        src_ref=src, dst_ref=dst, send_sem=send, recv_sem=recv, device_id=where, device_id_type=MESH
    )


def loop(low, high, body):
    lax.fori_loop(low, high, lambda i, c: (body(i), c)[1], 0)


def kernel(
    d,
    counts, slots, act, grads, basis_in, basis_out, eig,
    scaled_out, scores_out,
    g_all, b_out, onehot, valid, part, rs_first, rs_right, rs_left, y_mine, y_other, rot,
    basis_all, act_all, rot_act, masked, queries, eig_v, acc, sa, sb,
    loc, g_send, g_recv, f_send, f_recv, b_send, b_recv, a_send, a_recv,
    rs_send, rs_recv, y_send, y_recv, ag_send, ag_recv, ra_send, ra_recv,
    sa_send, sa_recv, sb_send, sb_recv,
):
    L, O, X, Z = d["L"], d["O"], d["X"], d["Z"]
    T, E, rows, CT, QR = d["T"], d["E"], d["rows"], d["CT"], d["QR"]
    CH, cuts = d["CH"], d["cuts"]
    F = E - QUERIES
    N = len(cuts)
    HR = Z // 2
    HL = Z - 1 - HR
    me_l, me_o = lax.axis_index("loop"), lax.axis_index("out")
    chip, x = me_l // 2, me_l // 4
    core, yh = me_l - 2 * chip, chip - 2 * x
    z = me_o // 2
    yl = me_o - 2 * z
    partner = me_l + 1 - 2 * core
    y_peer = me_o + 1 - 2 * yl

    def wrap(v, n):
        return jnp.where(v >= n, v - n, v)

    xs = [wrap(x + k, X) for k in range(X)]
    ys = [yh, 1 - yh]
    cs = [core, 1 - core]

    def to_loop(r):
        return (xs[r // 4] * 2 + ys[r // 2 % 2]) * 2 + cs[r % 2]

    def from_loop(r):
        return (xs[-(r // 4) % X] * 2 + ys[r // 2 % 2]) * 2 + cs[r % 2]

    def ring(k):
        v = z + k
        return wrap(jnp.where(v < 0, v + Z, v), Z)

    sides = [ring(1) * 2 + yl, ring(-1) * 2 + yl]
    outs = [wrap(me_o + k, O) for k in range(O)]

    own_g = pltpu.make_async_copy(grads, g_all.at[me_l], loc.at[0])
    own_act = pltpu.make_async_copy(act, act_all.at[core], loc.at[1])
    own_b = pltpu.make_async_copy(basis_out, b_out, loc.at[2])
    own_eig = pltpu.make_async_copy(eig, eig_v, loc.at[3])
    half = basis_all.shape[2]

    def columns(c):
        return pl.ds(pl.multiple_of(c * half, half), half)

    own_basis = pltpu.make_async_copy(basis_in.at[:, columns(core)], basis_all.at[me_l], loc.at[4])

    barrier = pltpu.get_barrier_semaphore()
    for r in range(1, L):
        pl.semaphore_signal(barrier, inc=1, device_id={"loop": to_loop(r)}, device_id_type=MESH)
    near = sides + [y_peer]
    for peer in near:
        pl.semaphore_signal(barrier, inc=1, device_id={"out": peer}, device_id_type=MESH)
    for copy in (own_g, own_b, own_act, own_eig, own_basis):
        copy.start()
    pl.semaphore_wait(barrier, L - 1 + len(near))

    shards = L // 2

    low = rows // 32 * 16
    splits = [(0, low), (low, rows - low)] if low else [(0, rows)]
    G = len(splits)

    def g_copy(r, p):
        cut = pl.ds(*splits[p])
        return remote(grads.at[cut], g_all.at[me_l, cut], g_send, g_recv.at[r, p], loop=to_loop(2 * r))

    def g_landed(r, p):
        here = g_all.at[from_loop(2 * r), pl.ds(*splits[p])]
        return remote(here, here, g_send, g_recv.at[r, p], loop=partner)

    def g_forward(r, p):
        here = g_all.at[from_loop(2 * r), pl.ds(*splits[p])]
        return remote(here, here, f_send, f_recv, loop=partner)

    for p in range(G):
        for r in range(shards - 1, 0, -1):
            g_copy(r, p).start()
    remote(grads, g_all.at[me_l], f_send, f_recv, loop=partner).start()

    which, position = slots[0:1, :], slots[1:2, :]
    target = jnp.full(which.shape, -1, jnp.int32)
    starts = []
    first = jnp.int32(0)
    for e in range(E):
        count = counts[e]
        target = jnp.where((which == e) & (position < count), position + first, target)
        starts.append(first)
        first = first + count
    starts.append(first)
    PB = d["PB"]

    def fill(i):
        at = pl.multiple_of(i * PB, PB)
        row = lax.broadcasted_iota(jnp.int32, (PB, which.shape[1]), 0) + at
        onehot[pl.ds(at, PB), :] = jnp.where(row == target, 1.0, 0.0).astype(BF16)

    loop(0, T // PB, fill)
    if Z * CH > CT * T:
        part[CT * T:, :] = jnp.zeros((Z * CH - CT * T, 128), F32)

    for p in range(G):
        for r in range(shards - 1, 0, -1):
            g_landed(r, p).wait_recv()
            g_forward(r, p).start()

    def basis_copy(r):
        return remote(basis_in.at[:, columns(cs[r % 2])], basis_all.at[me_l], b_send, b_recv.at[r], loop=to_loop(r))

    def basis_landed(r):
        src = from_loop(r)
        return remote(basis_all.at[src], basis_all.at[src], b_send, b_recv.at[r], loop=partner)

    def whole(ref, send, recv):
        return remote(ref, ref, send, recv, loop=partner)

    g_sent = whole(g_all.at[pl.ds(0, shards - 1)], g_send, g_recv.at[0, 0])
    forwards = whole(g_all.at[pl.ds(0, shards)], f_send, f_recv)
    act_copy = remote(act, act_all.at[core], a_send, a_recv, loop=partner)
    act_copy.start()
    if shards > 1:
        g_sent.wait_send()
    for r in range(L - 1, 0, -1):
        basis_copy(r).start()
    own_g.wait()
    forwards.wait_recv()

    MB = d["MB"]

    def compact(i):
        cut = pl.ds(pl.multiple_of(i * MB, MB), MB)
        tall = g_all[...].reshape(L * rows, g_all.shape[2])
        valid[cut, :] = jnp.dot(onehot[cut, :], tall, preferred_element_type=F32).astype(BF16)

    loop(0, T // MB, compact)
    own_b.wait()

    def product(j):
        tile = pl.ds(pl.multiple_of(j * 128, 128), 128)

        def block(i):
            at = pl.multiple_of(i * MB, MB)
            part[pl.ds(pl.multiple_of(j * T + at, 16), MB), :] = jnp.dot(
                valid[pl.ds(at, MB), :], b_out[:, tile], preferred_element_type=F32)

        loop(0, T // MB, block)

    def each_chunk(j, begin, step_of, merge):
        low, high = (j * T) // CH, (j * T + T - 1) // CH
        value = jnp.int32(begin)
        for k in range((T - 2) // CH + 2):
            ahead = jnp.minimum(low + k, high) - z
            value = merge(value, step_of(jnp.where(ahead < 0, ahead + Z, ahead)))
        return value

    def wanted(ahead):
        return jnp.where(ahead == 0, HR, jnp.where(ahead <= HR, HR - ahead, ahead - HR - 1))

    def products(s):
        def when_due(j):
            @pl.when(each_chunk(j, HR, wanted, jnp.minimum) == s)
            def _():
                product(j)

        loop(0, CT, when_due)

    inboxes = (rs_right, rs_left)

    def rows_of(chunk, u):
        return pl.ds(pl.multiple_of(chunk * CH + cuts[u][0], 16), cuts[u][1])

    def rs_copy(way, s, u):
        cut = pl.ds(*cuts[u])
        source = rs_first.at[way, cut] if s == 0 else inboxes[way].at[s - 1, cut]
        return remote(source, inboxes[way].at[s, cut], rs_send.at[way], rs_recv.at[way, s * N + u], out=sides[way])

    def rs_step(way, s, u):
        cut = pl.ds(*cuts[u])
        dest = rows_of(ring(HR - s) if way == 0 else ring(s - HL), u)
        if s == 0:
            rs_first[way, cut, :] = part[dest, :]
        else:
            rs_copy(way, s - 1, u).wait_recv()
            inboxes[way][s - 1, cut, :] = inboxes[way][s - 1, cut, :] + part[dest, :]
        rs_copy(way, s, u).start()

    depth = basis_in.shape[0]
    order = [0] + list(range(L - 1, 0, -1))
    rotated = [jnp.zeros((2 * rows, half), F32)]

    def rotate():
        r = order.pop(0)
        if r == 0:
            own_basis.wait()
            own_act.wait()
            act_copy.wait_recv()
        else:
            basis_landed(r).wait_recv()
        src = from_loop(r)
        a = act_all[:, :, pl.ds(pl.multiple_of(src * depth, depth), depth)].reshape(2 * rows, depth)
        rotated[0] = rotated[0] + jnp.dot(a, basis_all[src], preferred_element_type=F32)

    def ra_copy(r):
        place = rot_act.at[chip, :, columns(core)]
        return remote(place, place, ra_send, ra_recv, loop=to_loop(r))

    products(0)
    late = max(HR - -(-L // (2 * N)), 0)
    for s in range(HR):
        for u in range(N):
            rs_step(0, s, u)
            if s < HL:
                rs_step(1, s, u)
            if s >= late and order:
                rotate()
        products(s + 1)
    rotations = whole(act_all.at[:, :, pl.ds(0, (L - 1) * half)], ra_send, ra_recv)

    def y_copy(u):
        cut = pl.ds(*cuts[u])
        return remote(y_mine.at[cut], y_other.at[cut], y_send.at[u], y_recv.at[u], out=y_peer)

    def ag_copy(way, s, u):
        place = rot.at[rows_of(ring(-s) if way == 0 else ring(s), u)]
        return remote(place, place, ag_send.at[way], ag_recv.at[way, s * N + u], out=sides[way])

    def ag_landed(way, s, u):
        place = rot.at[rows_of(ring(-1 - s) if way == 0 else ring(1 + s), u)]
        return remote(place, place, ag_send.at[way], ag_recv.at[way, s * N + u], out=sides[way])

    for u in range(N):
        cut = pl.ds(*cuts[u])
        total = part[rows_of(z, u), :]
        if HL:
            rs_copy(1, HL - 1, u).wait_recv()
            total = total + rs_left[HL - 1, cut, :]
        rs_copy(0, HR - 1, u).wait_recv()
        y_mine[cut, :] = total + rs_right[HR - 1, cut, :]
        y_copy(u).start()
    while order:
        rotate()
    for u in range(N):
        cut = pl.ds(*cuts[u])
        y_copy(u).wait_recv()
        rot[rows_of(z, u), :] = (y_mine[cut, :] + y_other[cut, :]).astype(BF16)
        ag_copy(0, 0, u).start()
        if HL:
            ag_copy(1, 0, u).start()
    rot_act[chip, :, columns(core)] = rotated[0].astype(BF16)
    for r in range(L - 1, 0, -1):
        ra_copy(r).start()

    def gather_valid():
        rotations.wait_recv()

        def pick(i):
            cut = pl.ds(pl.multiple_of(i * MB, MB), MB)
            panels = rot_act[...].reshape(L * rows, 2 * half)
            masked[cut, :] = jnp.dot(onehot[cut, :], panels, preferred_element_type=F32).astype(BF16)

        loop(0, T // MB, pick)
        row = lax.broadcasted_iota(jnp.int32, (QR, 2 * half), 0)
        top = masked[:QR, :]
        for q in range(QUERIES):
            own = (row >= starts[q]) & (row < starts[q + 1])
            queries[:, 2 * half * q:2 * half * (q + 1)] = jnp.where(own, top, jnp.zeros_like(top))
        acc[...] = jnp.zeros_like(acc)
        own_eig.wait()

    factor = 1.0 / d["slots"] ** 0.5
    W = 2 * half

    def finish(j):
        grad = rot[pl.ds(pl.multiple_of(j * T, 16), T), :]
        tile = pl.ds(pl.multiple_of(j * 128, 128), 128)
        outer = lax.dot_general(
            grad[:QR], queries[...], (((0,), (0,)), ((), ())), preferred_element_type=F32) * factor
        divisor = eig_v[tile, :] + damping
        parts = []
        for q in range(QUERIES):
            parts.append((outer[:, W * q:W * (q + 1)] / divisor).astype(BF16))
            scaled_out[q, tile, :] = parts[q]
        wide = lax.dot_general(
            masked[...], jnp.concatenate(parts, axis=0), (((1,), (1,)), ((), ())), preferred_element_type=F32)
        grad = grad.astype(F32)
        for q in range(QUERIES):
            acc[q] = acc[q] + wide[:, 128 * q:128 * (q + 1)] * grad

    first_hop = min(4, HR)

    def arrival(ahead):
        return jnp.where(ahead <= HL, ahead, Z - ahead)

    for s in range(1, HR + 1):
        for u in range(N):
            ag_landed(0, s - 1, u).wait_recv()
            if s < HR:
                ag_copy(0, s, u).start()
            if s <= HL:
                ag_landed(1, s - 1, u).wait_recv()
                if s < HL:
                    ag_copy(1, s, u).start()
        if s == min(3, HR):
            gather_valid()
        if s >= first_hop:

            def ready(j):
                @pl.when(each_chunk(j, first_hop, arrival, jnp.maximum) == s)
                def _():
                    finish(j)

            loop(0, CT, ready)

    row = lax.broadcasted_iota(jnp.int32, (T, 128), 0)
    lane = lax.broadcasted_iota(jnp.int32, (1, 128), 1)
    mine = [jnp.zeros((1, 128), F32) for q in range(QUERIES)]
    for f in range(F):
        own = (row >= starts[QUERIES + f]) & (row < starts[QUERIES + f + 1])
        for q in range(QUERIES):
            value = jnp.sum(jnp.sum(jnp.where(own, acc[q], 0.0), axis=0, keepdims=True), axis=1, keepdims=True)
            mine[q] = jnp.where(lane == f, value, mine[q])
    for q in range(QUERIES):
        sa[me_l, q:q + 1, :] = mine[q]

    for r in range(L - 1, 0, -1):
        remote(sa.at[me_l], sa.at[me_l], sa_send, sa_recv, loop=to_loop(r)).start()

    forwards.wait_send()
    whole(basis_all.at[pl.ds(0, L - 1)], b_send, b_recv.at[0]).wait_send()
    act_copy.wait_send()
    for way, hops in ((0, HR), (1, HL)):
        if hops:
            whole(inboxes[way].at[pl.ds(0, hops)], rs_send.at[way], rs_recv.at[way, 0]).wait_send()
            whole(rot.at[pl.ds(0, hops * CH)], ag_send.at[way], ag_recv.at[way, 0]).wait_send()
    for u in range(N):
        y_copy(u).wait_send()
    rotations.wait_send()

    sa_all = whole(sa.at[pl.ds(0, L - 1)], sa_send, sa_recv)
    sa_all.wait_recv()
    sb[me_o] = jnp.sum(sa[...], axis=0)
    for k in range(1, O):
        remote(sb.at[me_o], sb.at[me_o], sb_send, sb_recv, out=outs[k]).start()
    sa_all.wait_send()
    sb_all = whole(sb.at[pl.ds(0, O - 1)], sb_send, sb_recv)
    sb_all.wait_recv()
    total = jnp.sum(sb[...], axis=0) * (factor / d["cells"] ** 0.5)
    scores_out[...] = total[:, :F]
    sb_all.wait_send()


def build(mesh, valid, cells):
    L, O = mesh.shape["loop"], mesh.shape["out"]
    Z = O // 2

    def body(activations, out_grads, token_counts, basis_in, basis_out, eigenvalues):
        E, here, din = activations.shape
        feats, cols = basis_out.shape
        depth, wide = basis_in.shape
        rows = E * here
        slots = here * L
        T, CT = valid, cols // 128
        groups = -(-CT * T // (Z * 16))
        CH = groups * 16
        edges = [groups * u // PIECES * 16 for u in range(PIECES + 1)]
        cuts = [(a, b - a) for a, b in zip(edges, edges[1:]) if b > a]
        N = len(cuts)
        HR = Z // 2
        HL = max(Z - 1 - HR, 1)
        half = wide // 2
        d = dict(L=L, O=O, X=L // 4, Z=Z, T=T, E=E, rows=rows, CT=CT, QR=min(QUERIES * slots, T), CH=CH, cuts=cuts,
                 PB=80 if T % 80 == 0 else 16, MB=400 if T % 400 == 0 else 16, slots=slots, cells=cells)
        index = np.arange(L * rows)
        table = np.zeros((8, L * rows), np.int32)
        table[0] = index % rows // here
        table[1] = index // rows * here + index % here
        dma = pltpu.SemaphoreType.DMA
        F = E - QUERIES
        scratch = [
            pltpu.VMEM((L, rows, feats), BF16),
            pltpu.VMEM((feats, cols), BF16),
            pltpu.VMEM((T, L * rows), BF16),
            pltpu.VMEM((T, feats), BF16),
            pltpu.VMEM((Z * CH, 128), F32),
            pltpu.VMEM((2, CH, 128), F32),
            pltpu.VMEM((HR, CH, 128), F32),
            pltpu.VMEM((HL, CH, 128), F32),
            pltpu.VMEM((CH, 128), F32),
            pltpu.VMEM((CH, 128), F32),
            pltpu.VMEM((Z * CH, 128), BF16),
            pltpu.VMEM((L, depth, half), BF16),
            pltpu.VMEM((2, rows, din), BF16),
            pltpu.VMEM((L // 2, 2 * rows, wide), BF16),
            pltpu.VMEM((T, wide), BF16),
            pltpu.VMEM((d["QR"], QUERIES * wide), BF16),
            pltpu.VMEM((cols, wide), F32),
            pltpu.VMEM((QUERIES, T, 128), F32),
            pltpu.VMEM((L, QUERIES, 128), F32),
            pltpu.VMEM((O, QUERIES, 128), F32),
            dma((5,)),
            dma, dma((L // 2, 2)), dma, dma,
            dma, dma((L,)), dma, dma,
            dma((2,)), dma((2, HR * N)), dma((N,)), dma((N,)),
            dma((2,)), dma((2, HR * N)),
            dma, dma, dma, dma, dma, dma,
        ]
        hbm = pl.BlockSpec(memory_space=pl.ANY)
        vmem = pl.BlockSpec(memory_space=pltpu.VMEM)
        return pl.pallas_call(
            functools.partial(kernel, d),
            out_shape=(
                pltpu.VMEM((QUERIES, cols, wide), BF16),
                pltpu.VMEM((QUERIES, F), F32),
            ),
            in_specs=[pl.BlockSpec(memory_space=pltpu.SMEM), vmem, hbm, hbm, hbm, hbm, hbm],
            out_specs=(vmem, vmem),
            scratch_shapes=scratch,
            compiler_params=pltpu.CompilerParams(
                collective_id=0, has_side_effects=True, vmem_limit_bytes=56 * 1024 * 1024),
            cost_estimate=pl.CostEstimate(flops=6 * 10**9, bytes_accessed=6 * 10**6, transcendentals=0),
        )(token_counts, jnp.asarray(table), activations.reshape(rows, din), out_grads.reshape(rows, feats),
          basis_in, basis_out, eigenvalues)

    return jax.shard_map(
        body,
        mesh=mesh,
        in_specs=(
            P(None, "loop", None),
            P(None, "loop", "out"),
            P(),
            P("loop", "out"),
            P("out", "loop"),
            P("loop", "out"),
        ),
        out_specs=(P(None, "loop", "out"), P()),
        check_vma=False,
    )


def solution(mesh):
    return build(mesh, VALID, KS * DIN)
```

```python
import functools

import jax
import jax.numpy as jnp
import numpy as np
from jax import lax
from jax.experimental import pallas as pl
from jax.experimental.pallas import tpu as pltpu
from jax.sharding import PartitionSpec as P

DIN = 8192
KS = 14336
QUERIES = 2
VALID = 800
PIECES = 4
damping = 0.1

F32 = jnp.float32
BF16 = jnp.bfloat16
MESH = pl.DeviceIdType.MESH


def remote(src, dst, send, recv, **where):
    return pltpu.make_async_remote_copy(
        src_ref=src, dst_ref=dst, send_sem=send, recv_sem=recv, device_id=where, device_id_type=MESH
    )


def loop(low, high, body):
    lax.fori_loop(low, high, lambda i, c: (body(i), c)[1], 0)


def kernel(
    d,
    counts, slots, act, grads, basis_in, basis_out, eig,
    scaled_out, scores_out,
    g_first, g_second, b_out, onehot, valid, part, rs_right, rs_left, y_mine, y_other, rot,
    basis_all, act_all, rot_act, masked, queries, eig_v, acc, sa, sb,
    loc, g_send, g_recv, f_send, f_recv, b_send, b_recv, a_send, a_recv,
    rs_send, rs_recv, y_send, y_recv, ag_send, ag_recv, ra_send, ra_recv,
    sa_send, sa_recv, sb_send, sb_recv,
):
    L, O, X, Z = d["L"], d["O"], d["X"], d["Z"]
    T, E, rows, CT, QR = d["T"], d["E"], d["rows"], d["CT"], d["QR"]
    CH, cuts = d["CH"], d["cuts"]
    F = E - QUERIES
    N = len(cuts)
    HR = Z // 2
    HL = Z - 1 - HR
    me_l, me_o = lax.axis_index("loop"), lax.axis_index("out")
    chip, x = me_l // 2, me_l // 4
    core, yh = me_l - 2 * chip, chip - 2 * x
    z = me_o // 2
    yl = me_o - 2 * z
    partner = me_l + 1 - 2 * core
    y_peer = me_o + 1 - 2 * yl

    def wrap(v, n):
        return jnp.where(v >= n, v - n, v)

    xs = [wrap(x + k, X) for k in range(X)]
    ys = [yh, 1 - yh]
    cs = [core, 1 - core]

    def to_loop(r):
        return (xs[r // 4] * 2 + ys[r // 2 % 2]) * 2 + cs[r % 2]

    def from_loop(r):
        return (xs[-(r // 4) % X] * 2 + ys[r // 2 % 2]) * 2 + cs[r % 2]

    def ring(k):
        v = z + k
        return wrap(jnp.where(v < 0, v + Z, v), Z)

    sides = [ring(1) * 2 + yl, ring(-1) * 2 + yl]
    outs = [wrap(me_o + k, O) for k in range(O)]

    splits = d["splits"]
    boxes = (g_first, g_second)
    own_g = [
        pltpu.make_async_copy(grads.at[pl.ds(*splits[p])], boxes[p].at[me_l], loc.at[5 * p]) for p in range(2)
    ]
    own_act = pltpu.make_async_copy(act, act_all.at[core], loc.at[1])
    own_b = pltpu.make_async_copy(basis_out, b_out, loc.at[2])
    own_eig = pltpu.make_async_copy(eig, eig_v, loc.at[3])
    half = basis_all.shape[2]

    def columns(c):
        return pl.ds(pl.multiple_of(c * half, half), half)

    own_basis = pltpu.make_async_copy(basis_in.at[:, columns(core)], basis_all.at[me_l], loc.at[4])

    barrier = pltpu.get_barrier_semaphore()
    for r in range(1, L):
        pl.semaphore_signal(barrier, inc=1, device_id={"loop": to_loop(r)}, device_id_type=MESH)
    near = sides + [y_peer]
    for peer in near:
        pl.semaphore_signal(barrier, inc=1, device_id={"out": peer}, device_id_type=MESH)
    for copy in (*own_g, own_b, own_act, own_eig, own_basis):
        copy.start()
    pl.semaphore_wait(barrier, L - 1 + len(near))

    shards = L // 2

    def g_copy(r, p):
        cut = pl.ds(*splits[p])
        return remote(grads.at[cut], boxes[p].at[me_l], g_send, g_recv.at[r, p], loop=to_loop(2 * r))

    def g_landed(r, p):
        here = boxes[p].at[from_loop(2 * r)]
        return remote(here, here, g_send, g_recv.at[r, p], loop=partner)

    def g_forward(r, p):
        here = boxes[p].at[from_loop(2 * r)]
        return remote(here, here, f_send, f_recv.at[p], loop=partner)

    for p in range(2):
        for r in range(shards - 1, 0, -1):
            g_copy(r, p).start()
        remote(grads.at[pl.ds(*splits[p])], boxes[p].at[me_l], f_send, f_recv.at[p], loop=partner).start()

    which, position = slots[0:1, :], slots[1:2, :]
    target = jnp.full(which.shape, -1, jnp.int32)
    starts = []
    first = jnp.int32(0)
    for e in range(E):
        count = counts[e]
        target = jnp.where((which == e) & (position < count), position + first, target)
        starts.append(first)
        first = first + count
    starts.append(first)
    PB = d["PB"]

    def fill(i):
        at = pl.multiple_of(i * PB, PB)
        row = lax.broadcasted_iota(jnp.int32, (PB, which.shape[1]), 0) + at
        onehot[pl.ds(at, PB), :] = jnp.where(row == target, 1.0, 0.0).astype(BF16)

    loop(0, T // PB, fill)
    if Z * CH > CT * T:
        part[CT * T:, :] = jnp.zeros((Z * CH - CT * T, 128), F32)

    for p in range(2):
        for r in range(shards - 1, 0, -1):
            g_landed(r, p).wait_recv()
            g_forward(r, p).start()

    def basis_copy(r):
        return remote(basis_in.at[:, columns(cs[r % 2])], basis_all.at[me_l], b_send, b_recv.at[r], loop=to_loop(r))

    def basis_landed(r):
        src = from_loop(r)
        return remote(basis_all.at[src], basis_all.at[src], b_send, b_recv.at[r], loop=partner)

    def whole(ref, send, recv):
        return remote(ref, ref, send, recv, loop=partner)

    g_sent = whole(valid.at[pl.ds(0, rows * (shards - 1))], g_send, g_recv.at[0, 0])
    g_forwards_sent = whole(valid.at[pl.ds(0, rows * shards)], f_send, f_recv.at[0])
    act_copy = remote(act, act_all.at[core], a_send, a_recv, loop=partner)
    act_copy.start()
    if shards > 1:
        g_sent.wait_send()
    for r in range(L - 1, 0, -1):
        basis_copy(r).start()

    MB = d["MB"]
    edge = L * splits[0][1]
    for p in range(2):
        own_g[p].wait()
        whole(boxes[p].at[pl.ds(0, shards)], f_send, f_recv.at[p]).wait_recv()

        def compact(i):
            cut = pl.ds(pl.multiple_of(i * MB, MB), MB)
            tall = boxes[p][...].reshape(L * splits[p][1], grads.shape[1])
            chosen = onehot[cut, edge:] if p else onehot[cut, :edge]
            moved = jnp.dot(chosen, tall, preferred_element_type=F32).astype(BF16)
            valid[cut, :] = valid[cut, :] + moved if p else moved

        loop(0, T // MB, compact)
    own_b.wait()

    def product(j):
        tile = pl.ds(pl.multiple_of(j * 128, 128), 128)

        def block(i):
            at = pl.multiple_of(i * MB, MB)
            part[pl.ds(pl.multiple_of(j * T + at, 16), MB), :] = jnp.dot(
                valid[pl.ds(at, MB), :], b_out[:, tile], preferred_element_type=F32)

        loop(0, T // MB, block)

    def each_chunk(j, begin, step_of, merge):
        low, high = (j * T) // CH, (j * T + T - 1) // CH
        value = jnp.int32(begin)
        for k in range((T - 2) // CH + 2):
            ahead = jnp.minimum(low + k, high) - z
            value = merge(value, step_of(jnp.where(ahead < 0, ahead + Z, ahead)))
        return value

    def wanted(ahead):
        return jnp.where(ahead == 0, HR, jnp.where(ahead <= HR, HR - ahead, ahead - HR - 1))

    def products(s):
        def when_due(j):
            @pl.when(each_chunk(j, HR, wanted, jnp.minimum) == s)
            def _():
                product(j)

        loop(0, CT, when_due)

    inboxes = (rs_right, rs_left)

    def rows_of(chunk, u):
        return pl.ds(pl.multiple_of(chunk * CH + cuts[u][0], 16), cuts[u][1])

    def rs_copy(way, s, u):
        cut = pl.ds(*cuts[u])
        source = inboxes[way].at[s - 1, cut] if s else part.at[rows_of(ring(HR) if way == 0 else ring(-HL), u)]
        return remote(source, inboxes[way].at[s, cut], rs_send.at[way], rs_recv.at[way, s * N + u], out=sides[way])

    def rs_step(way, s, u):
        cut = pl.ds(*cuts[u])
        dest = rows_of(ring(HR - s) if way == 0 else ring(s - HL), u)
        if s:
            rs_copy(way, s - 1, u).wait_recv()
            inboxes[way][s - 1, cut, :] = inboxes[way][s - 1, cut, :] + part[dest, :]
        rs_copy(way, s, u).start()

    depth = basis_in.shape[0]
    order = [0] + list(range(L - 1, 0, -1))
    rotated = [jnp.zeros((2 * rows, half), F32)]

    def rotate():
        r = order.pop(0)
        if r == 0:
            own_basis.wait()
            own_act.wait()
            act_copy.wait_recv()
        else:
            basis_landed(r).wait_recv()
        src = from_loop(r)
        a = act_all[:, :, pl.ds(pl.multiple_of(src * depth, depth), depth)].reshape(2 * rows, depth)
        rotated[0] = rotated[0] + jnp.dot(a, basis_all[src], preferred_element_type=F32)

    def ra_copy(r):
        place = rot_act.at[chip, :, columns(core)]
        return remote(place, place, ra_send, ra_recv, loop=to_loop(r))

    products(0)
    late = max(HR - -(-L // (2 * N)), 0)
    for s in range(HR):
        for u in range(N):
            rs_step(0, s, u)
            if s < HL:
                rs_step(1, s, u)
            if s >= late and order:
                rotate()
        products(s + 1)
    rotations = whole(act_all.at[:, :, pl.ds(0, (L - 1) * half)], ra_send, ra_recv)

    def y_copy(u):
        cut = pl.ds(*cuts[u])
        return remote(y_mine.at[cut], y_other.at[cut], y_send.at[u], y_recv.at[u], out=y_peer)

    def ag_copy(way, s, u):
        place = rot.at[rows_of(ring(-s) if way == 0 else ring(s), u)]
        return remote(place, place, ag_send.at[way], ag_recv.at[way, s * N + u], out=sides[way])

    def ag_landed(way, s, u):
        place = rot.at[rows_of(ring(-1 - s) if way == 0 else ring(1 + s), u)]
        return remote(place, place, ag_send.at[way], ag_recv.at[way, s * N + u], out=sides[way])

    for u in range(N):
        cut = pl.ds(*cuts[u])
        total = part[rows_of(z, u), :]
        if HL:
            rs_copy(1, HL - 1, u).wait_recv()
            total = total + rs_left[HL - 1, cut, :]
        rs_copy(0, HR - 1, u).wait_recv()
        y_mine[cut, :] = total + rs_right[HR - 1, cut, :]
        y_copy(u).start()
    while order:
        rotate()
    for u in range(N):
        cut = pl.ds(*cuts[u])
        y_copy(u).wait_recv()
        rot[rows_of(z, u), :] = (y_mine[cut, :] + y_other[cut, :]).astype(BF16)
        ag_copy(0, 0, u).start()
        if HL:
            ag_copy(1, 0, u).start()
    rot_act[chip, :, columns(core)] = rotated[0].astype(BF16)
    for r in range(L - 1, 0, -1):
        ra_copy(r).start()

    def gather_valid():
        rotations.wait_recv()

        def pick(i):
            cut = pl.ds(pl.multiple_of(i * MB, MB), MB)
            panels = rot_act[...].reshape(L, rows, 2 * half)
            pieces = [panels[:, a:a + n].reshape(L * n, 2 * half) for a, n in splits]
            total = jnp.dot(onehot[cut, :edge], pieces[0], preferred_element_type=F32)
            total = total + jnp.dot(onehot[cut, edge:], pieces[1], preferred_element_type=F32)
            masked[cut, :] = total.astype(BF16)

        loop(0, T // MB, pick)
        row = lax.broadcasted_iota(jnp.int32, (QR, 2 * half), 0)
        top = masked[:QR, :]
        for q in range(QUERIES):
            own = (row >= starts[q]) & (row < starts[q + 1])
            queries[:, 2 * half * q:2 * half * (q + 1)] = jnp.where(own, top, jnp.zeros_like(top))
        acc[...] = jnp.zeros_like(acc)
        own_eig.wait()

    factor = 1.0 / d["slots"] ** 0.5
    W = 2 * half

    def finish(j):
        grad = rot[pl.ds(pl.multiple_of(j * T, 16), T), :]
        tile = pl.ds(pl.multiple_of(j * 128, 128), 128)
        outer = lax.dot_general(
            grad[:QR], queries[...], (((0,), (0,)), ((), ())), preferred_element_type=F32) * factor
        divisor = eig_v[tile, :] + damping
        parts = []
        for q in range(QUERIES):
            parts.append((outer[:, W * q:W * (q + 1)] / divisor).astype(BF16))
            scaled_out[q, tile, :] = parts[q]
        wide = lax.dot_general(
            masked[...], jnp.concatenate(parts, axis=0), (((1,), (1,)), ((), ())), preferred_element_type=F32)
        grad = grad.astype(F32)
        for q in range(QUERIES):
            acc[q] = acc[q] + wide[:, 128 * q:128 * (q + 1)] * grad

    first_hop = min(4, HR)

    def arrival(ahead):
        return jnp.where(ahead <= HL, ahead, Z - ahead)

    for s in range(1, HR + 1):
        for u in range(N):
            ag_landed(0, s - 1, u).wait_recv()
            if s < HR:
                ag_copy(0, s, u).start()
            if s <= HL:
                ag_landed(1, s - 1, u).wait_recv()
                if s < HL:
                    ag_copy(1, s, u).start()
        if s == min(3, HR):
            gather_valid()
        if s >= first_hop:

            def ready(j):
                @pl.when(each_chunk(j, first_hop, arrival, jnp.maximum) == s)
                def _():
                    finish(j)

            loop(0, CT, ready)

    row = lax.broadcasted_iota(jnp.int32, (T, 128), 0)
    lane = lax.broadcasted_iota(jnp.int32, (1, 128), 1)
    mine = [jnp.zeros((1, 128), F32) for q in range(QUERIES)]
    for f in range(F):
        own = (row >= starts[QUERIES + f]) & (row < starts[QUERIES + f + 1])
        for q in range(QUERIES):
            value = jnp.sum(jnp.sum(jnp.where(own, acc[q], 0.0), axis=0, keepdims=True), axis=1, keepdims=True)
            mine[q] = jnp.where(lane == f, value, mine[q])
    for q in range(QUERIES):
        sa[me_l, q:q + 1, :] = mine[q]

    for r in sorted(range(1, L), key=lambda r: -min(r // 4, X - r // 4) - r // 2 % 2 * 2):
        remote(sa.at[me_l], sa.at[me_l], sa_send, sa_recv, loop=to_loop(r)).start()

    g_forwards_sent.wait_send()
    whole(basis_all.at[pl.ds(0, L - 1)], b_send, b_recv.at[0]).wait_send()
    act_copy.wait_send()
    for way, hops in ((0, HR), (1, HL)):
        if hops:
            whole(inboxes[way].at[pl.ds(0, hops)], rs_send.at[way], rs_recv.at[way, 0]).wait_send()
            whole(rot.at[pl.ds(0, hops * CH)], ag_send.at[way], ag_recv.at[way, 0]).wait_send()
    for u in range(N):
        y_copy(u).wait_send()
    rotations.wait_send()

    sa_all = whole(sa.at[pl.ds(0, L - 1)], sa_send, sa_recv)
    sa_all.wait_recv()
    sb[me_o] = jnp.sum(sa[...], axis=0)
    for k in sorted(range(1, O), key=lambda k: -min(k, O - k)):
        remote(sb.at[me_o], sb.at[me_o], sb_send, sb_recv, out=outs[k]).start()
    sa_all.wait_send()
    sb_all = whole(sb.at[pl.ds(0, O - 1)], sb_send, sb_recv)
    sb_all.wait_recv()
    total = jnp.sum(sb[...], axis=0) * (factor / d["cells"] ** 0.5)
    scores_out[...] = total[:, :F]
    sb_all.wait_send()


def build(mesh, valid, cells):
    L, O = mesh.shape["loop"], mesh.shape["out"]
    Z = O // 2

    def body(activations, out_grads, token_counts, basis_in, basis_out, eigenvalues):
        E, here, din = activations.shape
        feats, cols = basis_out.shape
        depth, wide = basis_in.shape
        rows = E * here
        slots = here * L
        T, CT = valid, cols // 128
        groups = -(-CT * T // (Z * 16))
        CH = groups * 16
        edges = [groups * u // PIECES * 16 for u in range(PIECES + 1)]
        cuts = [(a, b - a) for a, b in zip(edges, edges[1:]) if b > a]
        N = len(cuts)
        HR = Z // 2
        HL = max(Z - 1 - HR, 1)
        half = wide // 2
        index = np.arange(L * rows)
        low = -(-rows // 32) * 16
        splits = [(0, low), (low, rows - low)]
        index = np.concatenate([index.reshape(L, rows)[:, a:a + n].ravel() for a, n in splits])
        table = np.zeros((8, L * rows), np.int32)
        table[0] = index % rows // here
        table[1] = index // rows * here + index % here
        d = dict(splits=splits, L=L, O=O, X=L // 4, Z=Z, T=T, E=E, rows=rows, CT=CT, QR=min(QUERIES * slots, T), CH=CH, cuts=cuts,
                 PB=80 if T % 80 == 0 else 16, MB=400 if T % 400 == 0 else 16, slots=slots, cells=cells)
        dma = pltpu.SemaphoreType.DMA
        F = E - QUERIES
        scratch = [
            pltpu.VMEM((L, low, feats), BF16),
            pltpu.VMEM((L, rows - low, feats), BF16),
            pltpu.VMEM((feats, cols), BF16),
            pltpu.VMEM((T, L * rows), BF16),
            pltpu.VMEM((T, feats), BF16),
            pltpu.VMEM((Z * CH, 128), F32),
            pltpu.VMEM((HR, CH, 128), F32),
            pltpu.VMEM((HL, CH, 128), F32),
            pltpu.VMEM((CH, 128), F32),
            pltpu.VMEM((CH, 128), F32),
            pltpu.VMEM((Z * CH, 128), BF16),
            pltpu.VMEM((L, depth, half), BF16),
            pltpu.VMEM((2, rows, din), BF16),
            pltpu.VMEM((L // 2, 2 * rows, wide), BF16),
            pltpu.VMEM((T, wide), BF16),
            pltpu.VMEM((d["QR"], QUERIES * wide), BF16),
            pltpu.VMEM((cols, wide), F32),
            pltpu.VMEM((QUERIES, T, 128), F32),
            pltpu.VMEM((L, QUERIES, 128), F32),
            pltpu.VMEM((O, QUERIES, 128), F32),
            dma((6,)),
            dma, dma((L // 2, 2)), dma, dma((2,)),
            dma, dma((L,)), dma, dma,
            dma((2,)), dma((2, HR * N)), dma((N,)), dma((N,)),
            dma((2,)), dma((2, HR * N)),
            dma, dma, dma, dma, dma, dma,
        ]
        hbm = pl.BlockSpec(memory_space=pl.ANY)
        vmem = pl.BlockSpec(memory_space=pltpu.VMEM)
        return pl.pallas_call(
            functools.partial(kernel, d),
            out_shape=(
                pltpu.VMEM((QUERIES, cols, wide), BF16),
                pltpu.VMEM((QUERIES, F), F32),
            ),
            in_specs=[pl.BlockSpec(memory_space=pltpu.SMEM), vmem, hbm, hbm, hbm, hbm, hbm],
            out_specs=(vmem, vmem),
            scratch_shapes=scratch,
            compiler_params=pltpu.CompilerParams(
                collective_id=0, has_side_effects=True, vmem_limit_bytes=56 * 1024 * 1024),
            cost_estimate=pl.CostEstimate(flops=6 * 10**9, bytes_accessed=6 * 10**6, transcendentals=0),
        )(token_counts, jnp.asarray(table), activations.reshape(rows, din), out_grads.reshape(rows, feats),
          basis_in, basis_out, eigenvalues)

    return jax.shard_map(
        body,
        mesh=mesh,
        in_specs=(
            P(None, "loop", None),
            P(None, "loop", "out"),
            P(),
            P("loop", "out"),
            P("out", "loop"),
            P("loop", "out"),
        ),
        out_specs=(P(None, "loop", "out"), P()),
        check_vma=False,
    )


def solution(mesh):
    return build(mesh, VALID, KS * DIN)
```

```python
import functools

import jax
import jax.numpy as jnp
import numpy as np
from jax import lax
from jax.experimental import pallas as pl
from jax.experimental.pallas import tpu as pltpu
from jax.sharding import PartitionSpec as P

DIN = 8192
KS = 14336
QUERIES = 2
VALID = 800
PIECES = 4
damping = 0.1

F32 = jnp.float32
BF16 = jnp.bfloat16
MESH = pl.DeviceIdType.MESH


def remote(src, dst, send, recv, **where):
    return pltpu.make_async_remote_copy(
        src_ref=src, dst_ref=dst, send_sem=send, recv_sem=recv, device_id=where, device_id_type=MESH
    )


def loop(low, high, body):
    lax.fori_loop(low, high, lambda i, c: (body(i), c)[1], 0)


def kernel(
    d,
    counts, slots, act, grads, basis_in, basis_out, eig,
    scaled_out, scores_out,
    g_first, g_second, b_out, onehot, valid, part, rs_right, rs_left, y_mine, y_other, rot,
    basis_all, act_all, rot_act, masked, queries, eig_v, acc, sa, sb,
    loc, g_send, g_recv, f_send, f_recv, b_send, b_recv, a_send, a_recv,
    rs_send, rs_recv, y_send, y_recv, ag_send, ag_recv, ra_send, ra_recv,
    sa_send, sa_recv, sb_send, sb_recv,
):
    L, O, X, Z = d["L"], d["O"], d["X"], d["Z"]
    T, E, rows, CT, QR = d["T"], d["E"], d["rows"], d["CT"], d["QR"]
    CH, cuts = d["CH"], d["cuts"]
    F = E - QUERIES
    N = len(cuts)
    HR = Z // 2
    HL = Z - 1 - HR
    me_l, me_o = lax.axis_index("loop"), lax.axis_index("out")
    chip, x = me_l // 2, me_l // 4
    core, yh = me_l - 2 * chip, chip - 2 * x
    z = me_o // 2
    yl = me_o - 2 * z
    partner = me_l + 1 - 2 * core
    y_peer = me_o + 1 - 2 * yl

    def wrap(v, n):
        return jnp.where(v >= n, v - n, v)

    xs = [wrap(x + k, X) for k in range(X)]
    ys = [yh, 1 - yh]
    cs = [core, 1 - core]

    def to_loop(r):
        return (xs[r // 4] * 2 + ys[r // 2 % 2]) * 2 + cs[r % 2]

    def from_loop(r):
        return (xs[-(r // 4) % X] * 2 + ys[r // 2 % 2]) * 2 + cs[r % 2]

    def ring(k):
        v = z + k
        return wrap(jnp.where(v < 0, v + Z, v), Z)

    sides = [ring(1) * 2 + yl, ring(-1) * 2 + yl]
    outs = [wrap(me_o + k, O) for k in range(O)]

    splits = d["splits"]
    boxes = (g_first, g_second)
    own_g = [
        pltpu.make_async_copy(grads.at[pl.ds(*splits[p])], boxes[p].at[me_l], loc.at[5 * p]) for p in range(2)
    ]
    own_act = pltpu.make_async_copy(act, act_all.at[core], loc.at[1])
    own_b = pltpu.make_async_copy(basis_out, b_out, loc.at[2])
    own_eig = pltpu.make_async_copy(eig, eig_v, loc.at[3])
    half = basis_all.shape[2]

    def columns(c):
        return pl.ds(pl.multiple_of(c * half, half), half)

    own_basis = pltpu.make_async_copy(basis_in.at[:, columns(core)], basis_all.at[me_l], loc.at[4])

    barrier = pltpu.get_barrier_semaphore()
    for r in range(1, L):
        pl.semaphore_signal(barrier, inc=1, device_id={"loop": to_loop(r)}, device_id_type=MESH)
    near = sides + [y_peer]
    for peer in near:
        pl.semaphore_signal(barrier, inc=1, device_id={"out": peer}, device_id_type=MESH)
    for copy in (*own_g, own_b, own_act, own_eig, own_basis):
        copy.start()
    pl.semaphore_wait(barrier, L - 1 + len(near))

    shards = L // 2

    def g_copy(r, p):
        cut = pl.ds(*splits[p])
        return remote(grads.at[cut], boxes[p].at[me_l], g_send, g_recv.at[r, p], loop=to_loop(2 * r))

    def g_landed(r, p):
        here = boxes[p].at[from_loop(2 * r)]
        return remote(here, here, g_send, g_recv.at[r, p], loop=partner)

    def g_forward(r, p):
        here = boxes[p].at[from_loop(2 * r)]
        return remote(here, here, f_send, f_recv.at[p], loop=partner)

    for p in range(2):
        for r in range(shards - 1, 0, -1):
            g_copy(r, p).start()
        remote(grads.at[pl.ds(*splits[p])], boxes[p].at[me_l], f_send, f_recv.at[p], loop=partner).start()

    which, position = slots[0:1, :], slots[1:2, :]
    target = jnp.full(which.shape, -1, jnp.int32)
    starts = []
    first = jnp.int32(0)
    for e in range(E):
        count = counts[e]
        target = jnp.where((which == e) & (position < count), position + first, target)
        starts.append(first)
        first = first + count
    starts.append(first)
    PB = d["PB"]

    def fill(i):
        at = pl.multiple_of(i * PB, PB)
        row = lax.broadcasted_iota(jnp.int32, (PB, which.shape[1]), 0) + at
        onehot[pl.ds(at, PB), :] = jnp.where(row == target, 1.0, 0.0).astype(BF16)

    loop(0, T // PB, fill)
    if Z * CH > CT * T:
        part[CT * T:, :] = jnp.zeros((Z * CH - CT * T, 128), F32)

    for p in range(2):
        for r in range(shards - 1, 0, -1):
            g_landed(r, p).wait_recv()
            g_forward(r, p).start()

    def basis_copy(r):
        return remote(basis_in.at[:, columns(cs[r % 2])], basis_all.at[me_l], b_send, b_recv.at[r], loop=to_loop(r))

    def basis_landed(r):
        src = from_loop(r)
        return remote(basis_all.at[src], basis_all.at[src], b_send, b_recv.at[r], loop=partner)

    def whole(ref, send, recv):
        return remote(ref, ref, send, recv, loop=partner)

    g_sent = whole(valid.at[pl.ds(0, rows * (shards - 1))], g_send, g_recv.at[0, 0])
    g_forwards_sent = whole(valid.at[pl.ds(0, rows * shards)], f_send, f_recv.at[0])
    act_copy = remote(act, act_all.at[core], a_send, a_recv, loop=partner)
    if shards > 1:
        g_sent.wait_send()
    for r in range(L - 1, 0, -1):
        basis_copy(r).start()

    MB = d["MB"]
    edge = L * splits[0][1]
    for p in range(2):
        own_g[p].wait()
        whole(boxes[p].at[pl.ds(0, shards)], f_send, f_recv.at[p]).wait_recv()

        def compact(i):
            cut = pl.ds(pl.multiple_of(i * MB, MB), MB)
            tall = boxes[p][...].reshape(L * splits[p][1], grads.shape[1])
            chosen = onehot[cut, edge:] if p else onehot[cut, :edge]
            moved = jnp.dot(chosen, tall, preferred_element_type=F32).astype(BF16)
            valid[cut, :] = valid[cut, :] + moved if p else moved

        loop(0, T // MB, compact)
    act_copy.start()
    own_b.wait()

    def product(j):
        tile = pl.ds(pl.multiple_of(j * 128, 128), 128)

        def block(i):
            at = pl.multiple_of(i * MB, MB)
            part[pl.ds(pl.multiple_of(j * T + at, 16), MB), :] = jnp.dot(
                valid[pl.ds(at, MB), :], b_out[:, tile], preferred_element_type=F32)

        loop(0, T // MB, block)

    def each_chunk(j, begin, step_of, merge):
        low, high = (j * T) // CH, (j * T + T - 1) // CH
        value = jnp.int32(begin)
        for k in range((T - 2) // CH + 2):
            ahead = jnp.minimum(low + k, high) - z
            value = merge(value, step_of(jnp.where(ahead < 0, ahead + Z, ahead)))
        return value

    def wanted(ahead):
        return jnp.where(ahead == 0, HR, jnp.where(ahead <= HR, HR - ahead, ahead - HR - 1))

    def products(s):
        def when_due(j):
            @pl.when(each_chunk(j, HR, wanted, jnp.minimum) == s)
            def _():
                product(j)

        loop(0, CT, when_due)

    inboxes = (rs_right, rs_left)

    def rows_of(chunk, u):
        return pl.ds(pl.multiple_of(chunk * CH + cuts[u][0], 16), cuts[u][1])

    def rs_copy(way, s, u):
        cut = pl.ds(*cuts[u])
        source = inboxes[way].at[s - 1, cut] if s else part.at[rows_of(ring(HR) if way == 0 else ring(-HL), u)]
        return remote(source, inboxes[way].at[s, cut], rs_send.at[way], rs_recv.at[way, s * N + u], out=sides[way])

    def rs_step(way, s, u):
        cut = pl.ds(*cuts[u])
        dest = rows_of(ring(HR - s) if way == 0 else ring(s - HL), u)
        if s:
            rs_copy(way, s - 1, u).wait_recv()
            inboxes[way][s - 1, cut, :] = inboxes[way][s - 1, cut, :] + part[dest, :]
        rs_copy(way, s, u).start()

    depth = basis_in.shape[0]
    order = [0] + list(range(L - 1, 0, -1))
    rotated = [jnp.zeros((2 * rows, half), F32)]

    def rotate():
        r = order.pop(0)
        if r == 0:
            own_basis.wait()
            own_act.wait()
            act_copy.wait_recv()
        else:
            basis_landed(r).wait_recv()
        src = from_loop(r)
        a = act_all[:, :, pl.ds(pl.multiple_of(src * depth, depth), depth)].reshape(2 * rows, depth)
        rotated[0] = rotated[0] + jnp.dot(a, basis_all[src], preferred_element_type=F32)

    def ra_copy(r):
        place = rot_act.at[chip, :, columns(core)]
        return remote(place, place, ra_send, ra_recv, loop=to_loop(r))

    products(0)
    late = max(HR - -(-L // (2 * N)), 0)
    for s in range(HR):
        for u in range(N):
            rs_step(0, s, u)
            if s < HL:
                rs_step(1, s, u)
            if s >= late and order:
                rotate()
        products(s + 1)
    rotations = whole(act_all.at[:, :, pl.ds(0, (L - 1) * half)], ra_send, ra_recv)

    def y_copy(u):
        cut = pl.ds(*cuts[u])
        return remote(y_mine.at[cut], y_other.at[cut], y_send.at[u], y_recv.at[u], out=y_peer)

    def ag_copy(way, s, u):
        place = rot.at[rows_of(ring(-s) if way == 0 else ring(s), u)]
        return remote(place, place, ag_send.at[way], ag_recv.at[way, s * N + u], out=sides[way])

    def ag_landed(way, s, u):
        place = rot.at[rows_of(ring(-1 - s) if way == 0 else ring(1 + s), u)]
        return remote(place, place, ag_send.at[way], ag_recv.at[way, s * N + u], out=sides[way])

    for u in range(N):
        cut = pl.ds(*cuts[u])
        total = part[rows_of(z, u), :]
        if HL:
            rs_copy(1, HL - 1, u).wait_recv()
            total = total + rs_left[HL - 1, cut, :]
        rs_copy(0, HR - 1, u).wait_recv()
        y_mine[cut, :] = total + rs_right[HR - 1, cut, :]
        y_copy(u).start()
    while order:
        rotate()
    for u in range(N):
        cut = pl.ds(*cuts[u])
        y_copy(u).wait_recv()
        rot[rows_of(z, u), :] = (y_mine[cut, :] + y_other[cut, :]).astype(BF16)
        ag_copy(0, 0, u).start()
        if HL:
            ag_copy(1, 0, u).start()
    rot_act[chip, :, columns(core)] = rotated[0].astype(BF16)
    for r in range(L - 1, 0, -1):
        ra_copy(r).start()

    def gather_valid():
        rotations.wait_recv()

        def pick(i):
            cut = pl.ds(pl.multiple_of(i * MB, MB), MB)
            panels = rot_act[...].reshape(L, rows, 2 * half)
            pieces = [panels[:, a:a + n].reshape(L * n, 2 * half) for a, n in splits]
            total = jnp.dot(onehot[cut, :edge], pieces[0], preferred_element_type=F32)
            total = total + jnp.dot(onehot[cut, edge:], pieces[1], preferred_element_type=F32)
            masked[cut, :] = total.astype(BF16)

        loop(0, T // MB, pick)
        row = lax.broadcasted_iota(jnp.int32, (QR, 2 * half), 0)
        top = masked[:QR, :]
        for q in range(QUERIES):
            own = (row >= starts[q]) & (row < starts[q + 1])
            queries[:, 2 * half * q:2 * half * (q + 1)] = jnp.where(own, top, jnp.zeros_like(top))
        acc[...] = jnp.zeros_like(acc)
        own_eig.wait()

    factor = 1.0 / d["slots"] ** 0.5
    W = 2 * half

    def finish(j):
        grad = rot[pl.ds(pl.multiple_of(j * T, 16), T), :]
        tile = pl.ds(pl.multiple_of(j * 128, 128), 128)
        outer = lax.dot_general(
            grad[:QR], queries[...], (((0,), (0,)), ((), ())), preferred_element_type=F32) * factor
        divisor = eig_v[tile, :] + damping
        parts = []
        for q in range(QUERIES):
            parts.append((outer[:, W * q:W * (q + 1)] / divisor).astype(BF16))
            scaled_out[q, tile, :] = parts[q]
        wide = lax.dot_general(
            masked[...], jnp.concatenate(parts, axis=0), (((1,), (1,)), ((), ())), preferred_element_type=F32)
        grad = grad.astype(F32)
        for q in range(QUERIES):
            acc[q] = acc[q] + wide[:, 128 * q:128 * (q + 1)] * grad

    first_hop = min(4, HR)

    def arrival(ahead):
        return jnp.where(ahead <= HL, ahead, Z - ahead)

    for s in range(1, HR + 1):
        for u in range(N):
            ag_landed(0, s - 1, u).wait_recv()
            if s < HR:
                ag_copy(0, s, u).start()
            if s <= HL:
                ag_landed(1, s - 1, u).wait_recv()
                if s < HL:
                    ag_copy(1, s, u).start()
        if s == min(3, HR):
            gather_valid()
        if s >= first_hop:

            def ready(j):
                @pl.when(each_chunk(j, first_hop, arrival, jnp.maximum) == s)
                def _():
                    finish(j)

            loop(0, CT, ready)

    row = lax.broadcasted_iota(jnp.int32, (T, 128), 0)
    lane = lax.broadcasted_iota(jnp.int32, (1, 128), 1)
    mine = [jnp.zeros((1, 128), F32) for q in range(QUERIES)]
    for f in range(F):
        own = (row >= starts[QUERIES + f]) & (row < starts[QUERIES + f + 1])
        for q in range(QUERIES):
            value = jnp.sum(jnp.sum(jnp.where(own, acc[q], 0.0), axis=0, keepdims=True), axis=1, keepdims=True)
            mine[q] = jnp.where(lane == f, value, mine[q])
    for q in range(QUERIES):
        sa[me_l, q:q + 1, :] = mine[q]

    for r in sorted(range(1, L), key=lambda r: -min(r // 4, X - r // 4) - r // 2 % 2 * 2):
        remote(sa.at[me_l], sa.at[me_l], sa_send, sa_recv, loop=to_loop(r)).start()

    g_forwards_sent.wait_send()
    whole(basis_all.at[pl.ds(0, L - 1)], b_send, b_recv.at[0]).wait_send()
    act_copy.wait_send()
    for way, hops in ((0, HR), (1, HL)):
        if hops:
            whole(inboxes[way].at[pl.ds(0, hops)], rs_send.at[way], rs_recv.at[way, 0]).wait_send()
            whole(rot.at[pl.ds(0, hops * CH)], ag_send.at[way], ag_recv.at[way, 0]).wait_send()
    for u in range(N):
        y_copy(u).wait_send()
    rotations.wait_send()

    sa_all = whole(sa.at[pl.ds(0, L - 1)], sa_send, sa_recv)
    sa_all.wait_recv()
    sb[me_o] = jnp.sum(sa[...], axis=0)
    for k in sorted(range(1, O), key=lambda k: -min(k, O - k)):
        remote(sb.at[me_o], sb.at[me_o], sb_send, sb_recv, out=outs[k]).start()
    sa_all.wait_send()
    sb_all = whole(sb.at[pl.ds(0, O - 1)], sb_send, sb_recv)
    sb_all.wait_recv()
    total = jnp.sum(sb[...], axis=0) * (factor / d["cells"] ** 0.5)
    scores_out[...] = total[:, :F]
    sb_all.wait_send()


def build(mesh, valid, cells):
    L, O = mesh.shape["loop"], mesh.shape["out"]
    Z = O // 2

    def body(activations, out_grads, token_counts, basis_in, basis_out, eigenvalues):
        E, here, din = activations.shape
        feats, cols = basis_out.shape
        depth, wide = basis_in.shape
        rows = E * here
        slots = here * L
        T, CT = valid, cols // 128
        groups = -(-CT * T // (Z * 16))
        CH = groups * 16
        edges = [groups * u // PIECES * 16 for u in range(PIECES + 1)]
        cuts = [(a, b - a) for a, b in zip(edges, edges[1:]) if b > a]
        N = len(cuts)
        HR = Z // 2
        HL = max(Z - 1 - HR, 1)
        half = wide // 2
        index = np.arange(L * rows)
        low = -(-rows // 32) * 16
        splits = [(0, low), (low, rows - low)]
        index = np.concatenate([index.reshape(L, rows)[:, a:a + n].ravel() for a, n in splits])
        table = np.zeros((8, L * rows), np.int32)
        table[0] = index % rows // here
        table[1] = index // rows * here + index % here
        d = dict(splits=splits, L=L, O=O, X=L // 4, Z=Z, T=T, E=E, rows=rows, CT=CT, QR=min(QUERIES * slots, T), CH=CH, cuts=cuts,
                 PB=80 if T % 80 == 0 else 16, MB=400 if T % 400 == 0 else 16, slots=slots, cells=cells)
        dma = pltpu.SemaphoreType.DMA
        F = E - QUERIES
        scratch = [
            pltpu.VMEM((L, low, feats), BF16),
            pltpu.VMEM((L, rows - low, feats), BF16),
            pltpu.VMEM((feats, cols), BF16),
            pltpu.VMEM((T, L * rows), BF16),
            pltpu.VMEM((T, feats), BF16),
            pltpu.VMEM((Z * CH, 128), F32),
            pltpu.VMEM((HR, CH, 128), F32),
            pltpu.VMEM((HL, CH, 128), F32),
            pltpu.VMEM((CH, 128), F32),
            pltpu.VMEM((CH, 128), F32),
            pltpu.VMEM((Z * CH, 128), BF16),
            pltpu.VMEM((L, depth, half), BF16),
            pltpu.VMEM((2, rows, din), BF16),
            pltpu.VMEM((L // 2, 2 * rows, wide), BF16),
            pltpu.VMEM((T, wide), BF16),
            pltpu.VMEM((d["QR"], QUERIES * wide), BF16),
            pltpu.VMEM((cols, wide), F32),
            pltpu.VMEM((QUERIES, T, 128), F32),
            pltpu.VMEM((L, QUERIES, 128), F32),
            pltpu.VMEM((O, QUERIES, 128), F32),
            dma((6,)),
            dma, dma((L // 2, 2)), dma, dma((2,)),
            dma, dma((L,)), dma, dma,
            dma((2,)), dma((2, HR * N)), dma((N,)), dma((N,)),
            dma((2,)), dma((2, HR * N)),
            dma, dma, dma, dma, dma, dma,
        ]
        hbm = pl.BlockSpec(memory_space=pl.ANY)
        vmem = pl.BlockSpec(memory_space=pltpu.VMEM)
        return pl.pallas_call(
            functools.partial(kernel, d),
            out_shape=(
                pltpu.VMEM((QUERIES, cols, wide), BF16),
                pltpu.VMEM((QUERIES, F), F32),
            ),
            in_specs=[pl.BlockSpec(memory_space=pltpu.SMEM), vmem, hbm, hbm, hbm, hbm, hbm],
            out_specs=(vmem, vmem),
            scratch_shapes=scratch,
            compiler_params=pltpu.CompilerParams(
                collective_id=0, has_side_effects=True, vmem_limit_bytes=56 * 1024 * 1024),
            cost_estimate=pl.CostEstimate(flops=6 * 10**9, bytes_accessed=6 * 10**6, transcendentals=0),
        )(token_counts, jnp.asarray(table), activations.reshape(rows, din), out_grads.reshape(rows, feats),
          basis_in, basis_out, eigenvalues)

    return jax.shard_map(
        body,
        mesh=mesh,
        in_specs=(
            P(None, "loop", None),
            P(None, "loop", "out"),
            P(),
            P("loop", "out"),
            P("out", "loop"),
            P("loop", "out"),
        ),
        out_specs=(P(None, "loop", "out"), P()),
        check_vma=False,
    )


def solution(mesh):
    return build(mesh, VALID, KS * DIN)
```
